512 devices in a mesh: gx: 16 (over y, core), gy: 8 (over z), gz: 4 (over x).
Axes of the slice: x: 4, y: 8, z: 8, core: 2. Of those that a mesh axis runs over, the one named last changes fastest.
Arguments:
- parcel_vel: float32 [65536, 3, 128], P(('gx', 'gy', 'gz')), may hold values from -6 to 6
- parcel_props: float32 [65536, 2, 128], P(('gx', 'gy', 'gz')), may hold values from 0.05 to 2
- fill_count: int32 [65536], P(('gx', 'gy', 'gz')), may hold values from 64 to 128
- owner_peer: int32 [65536, 1], P(('gx', 'gy', 'gz')), may hold values from 0 to 127; in each aligned block of 128 rows (0 to 127, 128 to 255, ...) at most 2 rows name the same one
- cell_offset: int32 [65536], P(('gx', 'gy', 'gz')), may hold values from 0 to 36124
- shell_weight: float32 [128, 128], replicated, may hold values from 0 to 0.015625
- gas_state: float32 [4, 256, 128, 512], P(None, 'gx', 'gy', 'gz'), may hold values from -6 to 6
Outputs:
- parcels_next: float32 [131072, 5, 128], P(('gx', 'gy', 'gz'))
- gas_next: float32 [4, 256, 128, 512], P(None, 'gx', 'gy', 'gz')
The draws below stay inside these ranges and needn't reach their ends.
Inputs may be any that keep to these rules, and one draw needn't show every extreme that they name: `owner_peer`: among the 128 blocks of one device no owner is named more than 2 times, a bound that some block reaches.
All inputs are finite; a program needn't handle non-finite values.
Results may differ from the reference program's by a relative error of at most 0.000068.
Values sent between devices are 32-bit elements; how exact they have to be, the bound alone decides.
No kernel may reach another device: no remote copies, remote signals or barrier semaphores. Data moves between devices by JAX's collectives and lax.ppermute only.
A program may use at most 128 MiB of HBM per device.

```python
import math
import jax
import jax.numpy as jnp
import numpy as np
from jax import lax

CX = 16
CY = 16
CZ = 128
PB = 128
SLOTS = 128
PATCH = 128
PEERS = 128
MOST = 2
BLOCKS = 65536
OFFS = 36125
NX = 256
NY = 128
NZ = 512
N_GX = 16
N_GY = 8
N_GZ = 4


def with_ends(result, rng, smallest, high):
    shape = result.shape
    spot = [jax.random.randint(jax.random.fold_in(rng, axis), (), 0, shape[axis]) for axis in range(len(shape))]
    result = result.at[tuple(spot)].set(smallest)
    longest = shape.index(max(shape))
    spot[longest] = (spot[longest] + 1) % shape[longest]
    return result.at[tuple(spot)].set(high)


def shard_levels(stream_key, extent, shards, least, largest):
    loudness = 1.0
    for dim, blocks in shards:
        steps = jax.random.uniform(jax.random.fold_in(jax.random.fold_in(stream_key, 6), dim), (blocks,), jnp.float32, least / len(shards), largest / len(shards))
        loudness = loudness * jnp.repeat(jnp.exp(steps), extent[dim] // blocks).reshape((-1,) + (1,) * (len(extent) - 1 - dim))
    return loudness


def shared_out(own_key, own, number, rows, number_of, top, most, slope):
    order = jax.random.permutation(own_key, number_of)
    packed, usual = shares(number_of, rows * top, most, slope, True), shares(number_of, rows * top, most, slope, False)
    places = jnp.arange(number_of)

    def named(tallies, offset_by):
        used = int((tallies > 0).sum())
        fixed = max(1, used // 4)
        shifted = fixed + (places - fixed + offset_by * (used - fixed)) % max(1, number_of - fixed)
        return jnp.zeros((number_of,), jnp.int32).at[order[jnp.where(places < fixed, places, shifted)]].set(jnp.asarray(tallies, jnp.int32))

    tallies = jnp.where(number % 4 == 0, named(packed, number // 4), named(usual, number - number // 4 - 1))
    mixed = jax.random.permutation(jax.random.fold_in(own, 3), number_of)
    giver, taker = mixed[0:number_of // 2 * 2:2], mixed[1:number_of // 2 * 2:2]
    room = jnp.minimum(tallies[giver] - 1, most - tallies[taker]) // 2
    room = jnp.where((giver == order[0]) | (taker == order[0]) | (tallies[taker] == 0), 0, jnp.maximum(room, 0))
    shifted = jax.random.randint(jax.random.fold_in(own, 4), (number_of // 2,), 0, 1 << 20) % (room + 1)
    tallies = tallies.at[giver].add(-shifted).at[taker].add(shifted)
    members = jnp.searchsorted(jnp.cumsum(tallies), jnp.arange(rows * top), side="right").astype(jnp.int32)
    listing = members.reshape(top, rows).T
    listing = listing[jax.random.permutation(jax.random.fold_in(own, 1), rows)]
    offset_by = jax.random.randint(jax.random.fold_in(own, 2), (rows, 1), 0, top)
    return jnp.take_along_axis(listing, (jnp.arange(top)[None, :] + offset_by) % top, axis=1)


def shares(count, total, reach, skew, full):
    portions = [(1 << 20) // math.isqrt(standing ** skew) + 1 for standing in range(1, count + 1)]
    largest = reach if full else min(reach, max(-(-total // count), total * portions[0] // sum(portions)))
    least = 1 if total - largest >= count - 1 else 0
    holding, surplus = [largest] + [least] * (count - 1), total - largest - least * (count - 1)
    while surplus > 0:
        movable = [i for i in range(1, count) if holding[i] < largest] or [i for i in range(1, count) if holding[i] < reach]
        mass, budget = sum([portions[i] for i in movable]), surplus
        for i in movable:
            more = min(reach - holding[i], max(1, budget * portions[i] // mass), surplus)
            holding[i] = holding[i] + more
            surplus = surplus - more
    return np.array(holding)


def noise(own_key, dims, spread, reach, pieces=(), held_as=jnp.bfloat16):
    values = spread * jax.random.normal(own_key, dims, jnp.float32)
    if pieces:
        values = values * shard_levels(own_key, dims, pieces, -0.22, 0.18)
    return jnp.clip(values, -reach, reach).astype(held_as)


def setup_inputs(seed: int = 0) -> dict:
    splits = jax.random.split(jax.random.key(seed), 8)
    parcel_vel = noise(splits[0], (BLOCKS, 3, SLOTS), 1.0, 6.0, ((0, 512),), jnp.float32)
    parcel_props = jnp.clip(jnp.exp(math.log(2.0) - 3.6888794 * jax.random.uniform(splits[1], (BLOCKS, 2, SLOTS), jnp.float32) ** shard_levels(splits[1], (BLOCKS, 2, SLOTS), ((0, 512),), -0.2, 0.2)), 0.05, 2.0)
    fill_count = with_ends(jax.random.randint(splits[2], (BLOCKS,), SLOTS // 2, SLOTS + 1), jax.random.fold_in(splits[2], 1), SLOTS // 2, SLOTS).astype(jnp.int32)
    owner_peer_keys = jax.random.split(jax.random.fold_in(splits[3], 1), BLOCKS // PB)
    owner_peer_turns = jax.random.permutation(jax.random.fold_in(splits[3], 3), BLOCKS // PB)
    owner_peer = jax.vmap(lambda own, number: shared_out(jax.random.fold_in(splits[3], 2), own, number, PB, PEERS, 1, MOST, 2))(owner_peer_keys, owner_peer_turns).reshape((BLOCKS, 1))
    cell_offset = with_ends(jax.random.randint(splits[4], (BLOCKS,), 0, OFFS), jax.random.fold_in(splits[4], 1), 0, OFFS - 1).astype(jnp.int32)
    shell_weight = jnp.clip(jax.random.uniform(splits[5], (SLOTS, PATCH), jnp.float32, 0.0, 0.015625), 0.0, 0.015625)
    gas_state = noise(splits[6], (4, NX, NY, NZ), 1.0, 6.0, ((1, 16), (2, 8), (3, 4)), jnp.float32)
    return dict(parcel_vel=parcel_vel, parcel_props=parcel_props, fill_count=fill_count, owner_peer=owner_peer, cell_offset=cell_offset, shell_weight=shell_weight, gas_state=gas_state)


TIME_STEP = 0.05
SETTLING = 1.0
DIFFUSION = (1.0, 1.0, 1.0, 0.5)


def shell_pattern(stride_y, stride_z):
    cells = jnp.arange(PATCH, dtype=jnp.int32)
    step_x = cells // 32
    step_y = (cells // 8) % 4
    step_z = cells % 8
    return (step_x * stride_y + step_y) * stride_z + step_z


def laplace_op(padded):
    inner = padded[:, 1:-1, 1:-1, 1:-1]
    beside_all = padded[:, 2:, 1:-1, 1:-1] + padded[:, :-2, 1:-1, 1:-1]
    beside_all = beside_all + padded[:, 1:-1, 2:, 1:-1] + padded[:, 1:-1, :-2, 1:-1]
    beside_all = beside_all + padded[:, 1:-1, 1:-1, 2:] + padded[:, 1:-1, 1:-1, :-2]
    return beside_all - 6.0 * inner


def parcel_update(gas_near, velocity, props, alive_mask, shell_weight):
    gas_at = jnp.einsum('kbc,sc->bks', gas_near, shell_weight, precision=lax.Precision.HIGHEST)
    parcel_mass = props[:, 0:1, :]
    relax_time = props[:, 1:2, :]
    drag_rate = TIME_STEP / relax_time
    settle = jnp.array([0.0, 0.0, SETTLING], jnp.float32)[None, :, None]
    vel_next = (velocity + drag_rate * gas_at - TIME_STEP * settle) / (1.0 + drag_rate)
    impulse = parcel_mass * drag_rate * (gas_at - vel_next)
    force = jnp.concatenate([-impulse, parcel_mass], axis=1) * alive_mask[:, None, :]
    deposit = jnp.einsum('bks,sc->kbc', force, shell_weight, precision=lax.Precision.HIGHEST)
    payload = jnp.concatenate([vel_next, props], axis=1) * alive_mask[:, None, :]
    return payload, deposit


def reference(parcel_vel, parcel_props, fill_count, owner_peer, cell_offset, shell_weight, gas_state):
    peer_count = N_GX * N_GY
    stride_y = NY + 4
    stride_z = NZ + 4
    sender = jnp.arange(BLOCKS, dtype=jnp.int32) // PB
    target = owner_peer[:, 0]
    layer_index = sender % N_GZ
    anchor_x = (target // N_GY) * CX
    anchor_y = (target % N_GY) * CY
    anchor_z = layer_index * CZ
    offset_z = cell_offset % (CZ - 3)
    remain = cell_offset // (CZ - 3)
    offset_y = remain % (CY + 1)
    offset_x = remain // (CY + 1)
    shell_base = ((anchor_x + offset_x) * stride_y + anchor_y + offset_y) * stride_z + anchor_z + offset_z
    shell_index = (shell_base[:, None] + shell_pattern(stride_y, stride_z)[None, :]).astype(jnp.int32)
    padded = jnp.pad(gas_state, ((0, 0), (2, 2), (2, 2), (2, 2)))
    gas_near = padded[:3].reshape(3, -1)[:, shell_index]
    alive_mask = (jnp.arange(SLOTS, dtype=jnp.int32)[None, :] < fill_count[:, None]).astype(jnp.float32)
    payload, deposit = parcel_update(gas_near, parcel_vel, parcel_props, alive_mask, shell_weight)
    deposit_grid = jnp.zeros((4, padded[0].size), jnp.float32).at[:, shell_index].add(deposit)
    source = deposit_grid.reshape(padded.shape)[:, 2:-2, 2:-2, 2:-2]
    rates = jnp.array(DIFFUSION, jnp.float32)[:, None, None, None]
    gas_next = gas_state + TIME_STEP * rates * laplace_op(padded[:, 1:-1, 1:-1, 1:-1]) + source
    one_hot = (target.reshape(BLOCKS // PB, PB)[:, :, None] == jnp.arange(peer_count, dtype=jnp.int32)[None, None, :]).astype(jnp.int32)
    slot_rank = jnp.sum(one_hot * (jnp.cumsum(one_hot, axis=1) - 1), axis=2).reshape(BLOCKS)
    receiver = target * N_GZ + layer_index
    place = (receiver * (peer_count * MOST) + (sender // N_GZ) * MOST + slot_rank).astype(jnp.int32)
    total_rows = (BLOCKS // PB) * peer_count * MOST
    parcels_next = jnp.zeros((total_rows, 5, SLOTS), jnp.float32).at[place].set(payload)
    return parcels_next, gas_next
```

```python
import functools
import jax
import jax.numpy as jnp
from jax import lax
from jax.experimental import pallas as pl
from jax.experimental.pallas import tpu as pltpu
from jax.sharding import PartitionSpec as P

TIME_STEP = 0.05
SETTLING = 1.0
F32 = jnp.float32
BF16 = jnp.bfloat16
HI = lax.Precision.HIGHEST

LANES = 128
ROWS = 11
ZR = 144
ZO = 8
YS = 32


def iota(shape, dim):
    return lax.broadcasted_iota(jnp.int32, shape, dim)


def pack_kernel(tgt_ref, off_ref, cnt_ref, vel_ref, prop_ref, out_ref):
    n = LANES
    hot = (iota((n, n), 0) == tgt_ref[...]).astype(F32)
    earlier = (iota((n, n), 0) < iota((n, n), 1)).astype(BF16)
    rank = jnp.dot(hot.astype(BF16), earlier, preferred_element_type=F32)
    first = jnp.where(rank < 0.5, hot, 0.0)
    second = jnp.where(rank > 0.5, hot, 0.0)
    off = off_ref[...].astype(F32)
    cnt = cnt_ref[...].astype(F32)
    lane = iota((n, n), 1)
    head = jnp.zeros((n, n), F32)
    for place, (pick, val) in enumerate(((first, off), (second, off), (first, cnt), (second, cnt))):
        column = jnp.sum(pick * val, axis=1, keepdims=True)
        head = jnp.where(lane == place, column, head)
    out_ref[pl.ds(10, n, stride=ROWS), :] = head
    picks = jnp.concatenate([first, second], axis=0).astype(BF16)
    for k in range(5):
        x = vel_ref[:, k, :] if k < 3 else prop_ref[:, k - 3, :]
        total = jnp.zeros((2 * n, n), F32)
        for _ in range(3):
            part = x.astype(BF16)
            x = x - part.astype(F32)
            total = total + jnp.dot(picks, part, preferred_element_type=F32)
        out_ref[pl.ds(k, n, stride=ROWS), :] = total[:n]
        out_ref[pl.ds(5 + k, n, stride=ROWS), :] = total[n:]


def turn_kernel(gas_ref, low_ref, high_ref, out_ref, buf):
    cells_x, cells_y = gas_ref.shape[1], gas_ref.shape[2]
    buf[...] = jnp.zeros_like(buf)
    for x in range(cells_x):
        for k in range(4):
            buf[x, k * YS : k * YS + 2, :] = low_ref[k, x]
            buf[x, k * YS + 2 : k * YS + 2 + cells_y, :] = gas_ref[k, x]
            buf[x, k * YS + 2 + cells_y : k * YS + 4 + cells_y, :] = high_ref[k, x]
    for x in range(cells_x):
        out_ref[x] = buf[x].T


def base_kernel(mid_ref, zl_ref, zh_ref, xl_ref, xh_ref, pad_ref, base_ref):
    cells_x, cells_z = mid_ref.shape[0], mid_ref.shape[1]
    last = ZO + cells_z
    pad_ref[0:2] = xl_ref[...]
    pad_ref[cells_x + 2 : cells_x + 4] = xh_ref[...]
    pad_ref[2 : cells_x + 2, ZO:last, :] = mid_ref[...]
    pad_ref[2 : cells_x + 2, ZO - 2 : ZO, :] = zl_ref[...]
    pad_ref[2 : cells_x + 2, last : last + 2, :] = zh_ref[...]
    lane = iota((cells_z, LANES), 1)
    inside = (lane % YS >= 2) & (lane % YS < 18)
    rate = jnp.where(lane < 3 * YS, TIME_STEP, 0.5 * TIME_STEP).astype(F32)
    base_ref[0:2] = jnp.zeros((2, ZR, LANES), F32)
    base_ref[cells_x + 2 : cells_x + 4] = jnp.zeros((2, ZR, LANES), F32)

    @pl.loop(2, cells_x + 2)
    def _(x):
        here = pad_ref[x, ZO:last, :]
        beside = pad_ref[x + 1, ZO:last, :] + pad_ref[x - 1, ZO:last, :]
        beside = beside + pltpu.roll(here, LANES - 1, 1) + pltpu.roll(here, 1, 1)
        beside = beside + pad_ref[x, ZO + 1 : last + 1, :] + pad_ref[x, ZO - 1 : last - 1, :]
        value = here + rate * (beside - 6.0 * here)
        base_ref[x, 0:ZO, :] = jnp.zeros((ZO, LANES), F32)
        base_ref[x, ZO:last, :] = jnp.where(inside, value, 0.0)
        base_ref[x, last:ZR, :] = jnp.zeros((ZR - last, LANES), F32)


def parcel_kernel(
    recv_ref, pad_ref, base_ref, wt_ref, w_ref, pay_ref, sum_ref, xlo_ref, xhi_ref, code_v, code_s, acc, sem
):
    planes = pad_ref.shape[0] // ZR
    n = LANES
    off = recv_ref[pl.ds(10, n, stride=ROWS), :]
    rest = jnp.floor((off + 0.5) * (1.0 / 125.0))
    oz = off - rest * 125.0
    ox = jnp.floor((rest + 0.5) * (1.0 / 17.0))
    oy = rest - ox * 17.0
    code = oy * 4096.0 + ox * float(ZR) + oz + float(ZO - 2)
    code_v[...] = code.T[0:8].astype(jnp.int32)
    copy = pltpu.make_async_copy(code_v, code_s, sem)
    copy.start()
    acc[...] = base_ref[...]
    copy.wait()

    lane8 = iota((8, n), 1)
    group = (lane8 % YS) // 4
    quad = lane8 % 4
    lane = iota((YS, n), 1)

    @pl.loop(0, 8)
    def _(s):
        rank = s // 4
        q0 = (s % 4) * YS

        def place(b):
            c = code_s[rank, q0 + b]
            return jnp.bitwise_and(c, 4095), lax.shift_right_logical(c, 12)

        merged = []
        for g in range(4):
            total = [None] * 4
            for b8 in range(8):
                at, oy_b = place(b8 * 4 + g)
                shift = jnp.bitwise_and(4 * b8 - oy_b, n - 1)
                mine = group == b8
                for a in range(4):
                    x = pltpu.roll(pad_ref[pl.ds(at + a * ZR, 8), :], shift, 1)
                    total[a] = jnp.where(mine, x, 0.0 if total[a] is None else total[a])
            merged.append(total)
        cells = []
        for e in range(4):
            for a in range(4):
                x = merged[0][a]
                out = pltpu.roll(x, -e % n, 1) if e else x
                for g in range(1, 4):
                    x = merged[g][a]
                    x = pltpu.roll(x, (g - e) % n, 1) if g != e else x
                    out = jnp.where(quad == g, x, out)
                cells.append(out)
        near = jnp.concatenate(cells, axis=0).T
        gas_at = jnp.dot(near, wt_ref[...], precision=HI, preferred_element_type=F32)

        row = q0 * ROWS + rank * 5

        def take(k):
            return recv_ref[pl.ds(row + k, YS, stride=ROWS), :]

        head = recv_ref[pl.ds(q0 * ROWS + 10, YS, stride=ROWS), :]
        count = jnp.where(rank == 0, head[:, 2:3], head[:, 3:4])
        alive = lane.astype(F32) < count
        mass = jnp.where(alive, take(3), 0.0)
        relax = jnp.where(alive, take(4), 1.0)
        drag = TIME_STEP / relax
        forces = []
        for k in range(3):
            gas = gas_at[k * YS : (k + 1) * YS]
            settle = TIME_STEP * SETTLING if k == 2 else 0.0
            vel = (take(k) + drag * gas - settle) / (1.0 + drag)
            forces.append(-(mass * drag * (gas - vel)))
            pay_ref[k, rank, pl.ds(q0, YS), :] = jnp.where(alive, vel, 0.0)
        pay_ref[3, rank, pl.ds(q0, YS), :] = mass
        pay_ref[4, rank, pl.ds(q0, YS), :] = jnp.where(alive, relax, 0.0)
        forces.append(mass)
        force = jnp.concatenate(forces, axis=0)
        spread = lax.dot_general(
            w_ref[...], force, (((1,), (1,)), ((), ())), precision=HI, preferred_element_type=F32
        )
        for g in range(4):
            parts = []
            for a in range(4):
                out = None
                for e in range(4):
                    x = spread[(e * 4 + a) * 8 : (e * 4 + a) * 8 + 8]
                    x = pltpu.roll(x, (e - g) % n, 1) if e != g else x
                    out = x if out is None else jnp.where(quad == e, x, out)
                parts.append(out)
            for b8 in range(8):
                at, oy_b = place(b8 * 4 + g)
                shift = jnp.bitwise_and(oy_b - 4 * b8, n - 1)
                mine = group == b8
                for a in range(4):
                    x = pltpu.roll(jnp.where(mine, parts[a], 0.0), shift, 1)
                    acc[pl.ds(at + a * ZR, 8), :] = acc[pl.ds(at + a * ZR, 8), :] + x

    sum_ref[...] = acc[2 * ZR : (planes - 2) * ZR, :]
    xlo_ref[...] = acc[0 : 2 * ZR, :]
    xhi_ref[...] = acc[(planes - 2) * ZR :, :]


def back_kernel(sum_ref, xl_ref, xh_ref, zl_ref, zh_ref, out_ref, ylo_ref, yhi_ref, buf):
    cells_x = sum_ref.shape[0]
    cells_z = out_ref.shape[3]
    cells_y = out_ref.shape[2]
    for x in range(cells_x):
        value = sum_ref[x, ZO : ZO + cells_z, :]
        if x < 2:
            value = value + xl_ref[x, ZO : ZO + cells_z, :]
        if x >= cells_x - 2:
            value = value + xh_ref[x - cells_x + 2, ZO : ZO + cells_z, :]
        buf[x] = value
    buf[:, 0:2, :] += zl_ref[...]
    buf[:, cells_z - 2 : cells_z, :] += zh_ref[...]
    for x in range(cells_x):
        flat = buf[x].T
        for k in range(4):
            out_ref[k, x] = flat[k * YS + 2 : k * YS + 2 + cells_y]
            ylo_ref[k, x] = flat[k * YS : k * YS + 2]
            yhi_ref[k, x] = flat[k * YS + 2 + cells_y : k * YS + 4 + cells_y]


def shift_pair(to_low, to_high, axis):
    count = lax.axis_size(axis)
    up = [(i, i + 1) for i in range(count - 1)]
    down = [(j, i) for i, j in up]
    return lax.ppermute(to_high, axis, up), lax.ppermute(to_low, axis, down)


def call(kernel, outs, scratch=(), cost=None, **kw):
    return pl.pallas_call(
        kernel,
        out_shape=outs,
        scratch_shapes=list(scratch),
        compiler_params=pltpu.CompilerParams(vmem_limit_bytes=40 * 2**20),
        cost_estimate=cost,
        **kw,
    )


def arr(*shape, dtype=F32):
    return jax.ShapeDtypeStruct(shape, dtype)


def per_device(parcel_vel, parcel_props, fill_count, owner_peer, cell_offset, shell_weight, gas_state):
    _, nx, ny, nz = gas_state.shape
    blocks = parcel_vel.shape[0]
    send = call(pack_kernel, arr(blocks * ROWS, LANES))(
        owner_peer.reshape(1, blocks),
        cell_offset.reshape(1, blocks),
        fill_count.reshape(1, blocks),
        parcel_vel,
        parcel_props,
    )
    recv = lax.all_to_all(
        send.reshape(blocks, ROWS * LANES), ("gx", "gy"), split_axis=0, concat_axis=0, tiled=True
    ).reshape(blocks * ROWS, LANES)

    y_low, y_high = shift_pair(gas_state[:, :, :2], gas_state[:, :, ny - 2 :], "gy")
    mid = call(turn_kernel, arr(nx, nz, LANES), [pltpu.VMEM((nx, LANES, nz), F32)])(gas_state, y_low, y_high)
    z_low, z_high = shift_pair(mid[:, :2], mid[:, nz - 2 :], "gz")

    def face(lo, hi):
        zero = jnp.zeros((2, ZO - 2, LANES), F32)
        return jnp.concatenate([zero, z_low[lo:hi], mid[lo:hi], z_high[lo:hi], zero], axis=1)

    x_low, x_high = shift_pair(face(0, 2), face(nx - 2, nx), "gx")
    padded, base = call(base_kernel, [arr(nx + 4, ZR, LANES)] * 2)(mid, z_low, z_high, x_low, x_high)

    weight = shell_weight.reshape(LANES, 4, 4, 8).transpose(2, 1, 3, 0).reshape(LANES, LANES)
    rows = (nx + 4) * ZR
    pay, total, x_lo, x_hi = call(
        parcel_kernel,
        [arr(5, 2, blocks, LANES), arr(nx * ZR, LANES), arr(2 * ZR, LANES), arr(2 * ZR, LANES)],
        [
            pltpu.VMEM((8, LANES), jnp.int32),
            pltpu.SMEM((8, LANES), jnp.int32),
            pltpu.VMEM((rows, LANES), F32),
            pltpu.SemaphoreType.DMA,
        ],
    )(recv, padded.reshape(rows, LANES), base.reshape(rows, LANES), weight, weight)
    parcels_next = pay.transpose(2, 1, 0, 3).reshape(2 * blocks, 5, LANES)

    from_low, from_high = shift_pair(x_lo.reshape(2, ZR, LANES), x_hi.reshape(2, ZR, LANES), "gx")
    total = total.reshape(nx, ZR, LANES)

    def rim(lo, hi):
        part = total[:, lo:hi]
        return jnp.concatenate(
            [part[:2] + from_low[:, lo:hi], part[2 : nx - 2], part[nx - 2 :] + from_high[:, lo:hi]], axis=0
        )

    z_below, z_above = shift_pair(rim(ZO - 2, ZO), rim(ZO + nz, ZO + nz + 2), "gz")
    rows_out, y_lo, y_hi = call(
        back_kernel,
        [arr(4, nx, ny, nz), arr(4, nx, 2, nz), arr(4, nx, 2, nz)],
        [pltpu.VMEM((nx, nz, LANES), F32)],
    )(total, from_low, from_high, z_below, z_above)
    y_below, y_above = shift_pair(y_lo, y_hi, "gy")
    gas_next = jnp.concatenate(
        [rows_out[:, :, :2] + y_below, rows_out[:, :, 2 : ny - 2], rows_out[:, :, ny - 2 :] + y_above], axis=2
    )
    return parcels_next, gas_next


def solution(mesh):
    return jax.shard_map(
        per_device,
        mesh=mesh,
        in_specs=(
            P(("gx", "gy", "gz"), None, None),
            P(("gx", "gy", "gz"), None, None),
            P(("gx", "gy", "gz")),
            P(("gx", "gy", "gz"), None),
            P(("gx", "gy", "gz")),
            P(),
            P(None, "gx", "gy", "gz"),
        ),
        out_specs=(P(("gx", "gy", "gz"), None, None), P(None, "gx", "gy", "gz")),
        check_vma=False,
    )
```

```python
import functools
import jax
import jax.numpy as jnp
from jax import lax
from jax.experimental import pallas as pl
from jax.experimental.pallas import tpu as pltpu
from jax.sharding import PartitionSpec as P

TIME_STEP = 0.05
SETTLING = 1.0
F32 = jnp.float32
BF16 = jnp.bfloat16
HI = lax.Precision.HIGHEST

LANES = 128
ROWS = 11
ZR = 144
ZO = 8
YS = 32


def iota(shape, dim):
    return lax.broadcasted_iota(jnp.int32, shape, dim)


def pack_kernel(tgt_ref, off_ref, cnt_ref, vel_ref, prop_ref, out_ref):
    n = LANES
    hot = (iota((n, n), 0) == tgt_ref[...]).astype(F32)
    earlier = (iota((n, n), 0) < iota((n, n), 1)).astype(BF16)
    rank = jnp.dot(hot.astype(BF16), earlier, preferred_element_type=F32)
    first = jnp.where(rank < 0.5, hot, 0.0)
    second = jnp.where(rank > 0.5, hot, 0.0)
    off = off_ref[...].astype(F32)
    cnt = cnt_ref[...].astype(F32)
    lane = iota((n, n), 1)
    head = jnp.zeros((n, n), F32)
    for place, (pick, val) in enumerate(((first, off), (second, off), (first, cnt), (second, cnt))):
        column = jnp.sum(pick * val, axis=1, keepdims=True)
        head = jnp.where(lane == place, column, head)
    out_ref[pl.ds(10, n, stride=ROWS), :] = head
    picks = jnp.concatenate([first, second], axis=0).astype(BF16)
    for k in range(5):
        x = vel_ref[k] if k < 3 else prop_ref[:, k - 3, :]
        total = jnp.zeros((2 * n, n), F32)
        for _ in range(3):
            part = x.astype(BF16)
            x = x - part.astype(F32)
            total = total + jnp.dot(picks, part, preferred_element_type=F32)
        out_ref[pl.ds(k, n, stride=ROWS), :] = total[:n]
        out_ref[pl.ds(5 + k, n, stride=ROWS), :] = total[n:]


def turn_kernel(gas_ref, low_ref, high_ref, send_ref, out_ref, same_ref, buf):
    del send_ref, same_ref
    cells_x, cells_y = gas_ref.shape[1], gas_ref.shape[2]
    buf[...] = jnp.zeros_like(buf)
    for x in range(cells_x):
        for k in range(4):
            buf[x, k * YS : k * YS + 2, :] = low_ref[k, x]
            buf[x, k * YS + 2 : k * YS + 2 + cells_y, :] = gas_ref[k, x]
            buf[x, k * YS + 2 + cells_y : k * YS + 4 + cells_y, :] = high_ref[k, x]
    for x in range(cells_x):
        out_ref[x] = buf[x].T


def diffuse_kernel(mid_ref, zl_ref, zh_ref, xl_ref, xh_ref, out_ref, col):
    cells_x, cells_z = mid_ref.shape[0], mid_ref.shape[1]
    last = ZO + cells_z
    lane = iota((cells_z, LANES), 1)
    rate = jnp.where(lane < 3 * YS, TIME_STEP, 0.5 * TIME_STEP).astype(F32)
    for x in range(cells_x):
        here = mid_ref[x]
        col[x % 2, ZO:last, :] = here
        col[x % 2, ZO - 2 : ZO, :] = zl_ref[x]
        col[x % 2, last : last + 2, :] = zh_ref[x]
        left = mid_ref[x - 1] if x else xl_ref[1, ZO:last, :]
        right = mid_ref[x + 1] if x < cells_x - 1 else xh_ref[0, ZO:last, :]
        beside = left + right + pltpu.roll(here, LANES - 1, 1) + pltpu.roll(here, 1, 1)
        beside = beside + col[x % 2, ZO + 1 : last + 1, :] + col[x % 2, ZO - 1 : last - 1, :]
        out_ref[x] = here + rate * (beside - 6.0 * here)


def parcel_kernel(
    recv_ref, mid_ref, zl_ref, zh_ref, xl_ref, xh_ref, w_ref,
    pay_ref, sum_ref, xlo_ref, xhi_ref,
    code_v, code_s, pad, acc, near, force, sem,
):
    cells_x, cells_z = mid_ref.shape[0], mid_ref.shape[1]
    planes = cells_x + 4
    last = ZO + cells_z
    n = LANES
    off = recv_ref[pl.ds(10, n, stride=ROWS), :]
    rest = jnp.floor((off + 0.5) * (1.0 / 125.0))
    oz = off - rest * 125.0
    ox = jnp.floor((rest + 0.5) * (1.0 / 17.0))
    oy = rest - ox * 17.0
    code = oy * 4096.0 + ox * float(ZR) + oz + float(ZO - 2)
    code_v[...] = code.T[0:8].astype(jnp.int32)
    copy = pltpu.make_async_copy(code_v, code_s, sem)
    copy.start()
    for p in range(2):
        pad[p * ZR : (p + 1) * ZR, :] = xl_ref[p]
        pad[(planes - 2 + p) * ZR : (planes - 1 + p) * ZR, :] = xh_ref[p]
    for x in range(cells_x):
        at = (x + 2) * ZR
        pad[at + ZO : at + last, :] = mid_ref[x]
        pad[at + ZO - 2 : at + ZO, :] = zl_ref[x]
        pad[at + last : at + last + 2, :] = zh_ref[x]
    acc[...] = jnp.zeros_like(acc)
    copy.wait()

    lane8 = iota((8, n), 1)
    group = (lane8 % YS) // 4
    quad = lane8 % 4
    lane = iota((YS, n), 1)

    def place(s, b):
        c = code_s[s // 4, (s % 4) * YS + b]
        return jnp.bitwise_and(c, 4095), lax.shift_right_logical(c, 12)

    @pl.loop(0, 8)
    def _(s):
        merged = []
        for g in range(4):
            total = [None] * 4
            for b8 in range(8):
                at, oy_b = place(s, b8 * 4 + g)
                shift = jnp.bitwise_and(4 * b8 - oy_b, n - 1)
                mine = group == b8
                for a in range(4):
                    x = pltpu.roll(pad[pl.ds(at + a * ZR, 8), :], shift, 1)
                    total[a] = jnp.where(mine, x, 0.0 if total[a] is None else total[a])
            merged.append(total)
        cells = []
        for e in range(4):
            for a in range(4):
                x = merged[0][a]
                out = pltpu.roll(x, -e % n, 1) if e else x
                for g in range(1, 4):
                    x = merged[g][a]
                    x = pltpu.roll(x, (g - e) % n, 1) if g != e else x
                    out = jnp.where(quad == g, x, out)
                cells.append(out)
        near[pl.ds(pl.multiple_of(s * n, n), n), :] = jnp.concatenate(cells, axis=0).T

    gas_all = jnp.dot(near[...], w_ref[...], precision=HI, preferred_element_type=F32)
    for s in range(8):
        rank, q0 = s // 4, (s % 4) * YS
        row = q0 * ROWS + rank * 5

        def take(k):
            return recv_ref[pl.ds(row + k, YS, stride=ROWS), :]

        head = recv_ref[pl.ds(q0 * ROWS + 10, YS, stride=ROWS), :]
        alive = lane.astype(F32) < head[:, 2 + rank : 3 + rank]
        mass = jnp.where(alive, take(3), 0.0)
        relax = jnp.where(alive, take(4), 1.0)
        drag = TIME_STEP / relax
        under = 1.0 / (1.0 + drag)
        slots = pl.ds(2 * q0 + rank, YS, stride=2)
        for k in range(3):
            gas = gas_all[s * n + k * YS : s * n + (k + 1) * YS]
            settle = TIME_STEP * SETTLING if k == 2 else 0.0
            vel = (take(k) + drag * gas - settle) * under
            force[s * n + k * YS : s * n + (k + 1) * YS, :] = -(mass * drag * (gas - vel))
            pay_ref[k, slots, :] = jnp.where(alive, vel, 0.0)
        pay_ref[3, slots, :] = mass
        pay_ref[4, slots, :] = jnp.where(alive, relax, 0.0)
        force[s * n + 3 * YS : (s + 1) * n, :] = mass
    for s in range(8):
        near[s * n : (s + 1) * n, :] = lax.dot_general(
            w_ref[...],
            force[s * n : (s + 1) * n, :],
            (((1,), (1,)), ((), ())),
            precision=HI,
            preferred_element_type=F32,
        )

    @pl.loop(0, 8)
    def _(s):
        spread = near[pl.ds(pl.multiple_of(s * n, n), n), :]
        for g in range(4):
            parts = []
            for a in range(4):
                out = None
                for e in range(4):
                    x = spread[(e * 4 + a) * 8 : (e * 4 + a) * 8 + 8]
                    x = pltpu.roll(x, (e - g) % n, 1) if e != g else x
                    out = x if out is None else jnp.where(quad == e, x, out)
                parts.append(out)
            for b8 in range(8):
                at, oy_b = place(s, b8 * 4 + g)
                shift = jnp.bitwise_and(oy_b - 4 * b8, n - 1)
                mine = group == b8
                adds = [pltpu.roll(jnp.where(mine, parts[a], 0.0), shift, 1) for a in range(4)]
                olds = [acc[pl.ds(at + a * ZR, 8), :] for a in range(4)]
                for a in range(4):
                    acc[pl.ds(at + a * ZR, 8), :] = olds[a] + adds[a]

    sum_ref[...] = acc[2 * ZR : (planes - 2) * ZR, :]
    xlo_ref[...] = acc[0 : 2 * ZR, :]
    xhi_ref[...] = acc[(planes - 2) * ZR :, :]


def back_kernel(sum_ref, base_ref, xl_ref, xh_ref, zl_ref, zh_ref, out_ref, ylo_ref, yhi_ref, buf):
    cells_x = sum_ref.shape[0]
    cells_z = out_ref.shape[3]
    cells_y = out_ref.shape[2]
    for x in range(cells_x):
        value = sum_ref[x, ZO : ZO + cells_z, :]
        if x < 2:
            value = value + xl_ref[x, ZO : ZO + cells_z, :]
        if x >= cells_x - 2:
            value = value + xh_ref[x - cells_x + 2, ZO : ZO + cells_z, :]
        buf[x] = value
    buf[:, 0:2, :] += zl_ref[...]
    buf[:, cells_z - 2 : cells_z, :] += zh_ref[...]
    lane = iota((cells_z, LANES), 1)
    inside = (lane % YS >= 2) & (lane % YS < 2 + cells_y)
    for x in range(cells_x):
        flat = (buf[x] + jnp.where(inside, base_ref[x], 0.0)).T
        for k in range(4):
            out_ref[k, x] = flat[k * YS + 2 : k * YS + 2 + cells_y]
            ylo_ref[k, x] = flat[k * YS : k * YS + 2]
            yhi_ref[k, x] = flat[k * YS + 2 + cells_y : k * YS + 4 + cells_y]


def shift_pair(to_low, to_high, axis):
    count = lax.axis_size(axis)
    up = [(i, i + 1) for i in range(count - 1)]
    down = [(j, i) for i, j in up]
    return lax.ppermute(to_high, axis, up), lax.ppermute(to_low, axis, down)


def call(kernel, outs, scratch=(), cost=None, **kw):
    return pl.pallas_call(
        kernel,
        out_shape=outs,
        scratch_shapes=list(scratch),
        compiler_params=pltpu.CompilerParams(vmem_limit_bytes=40 * 2**20),
        cost_estimate=cost,
        **kw,
    )


def arr(*shape, dtype=F32):
    return jax.ShapeDtypeStruct(shape, dtype)


def parcels(recv, mid, z_low, z_high, x_low, x_high, weight):
    nx = mid.shape[0]
    blocks = recv.shape[0] // ROWS
    rows = (nx + 4) * ZR
    return call(
        parcel_kernel,
        [arr(5, 2 * blocks, LANES), arr(nx * ZR, LANES), arr(2 * ZR, LANES), arr(2 * ZR, LANES)],
        [
            pltpu.VMEM((8, LANES), jnp.int32),
            pltpu.SMEM((8, LANES), jnp.int32),
            pltpu.VMEM((rows, LANES), F32),
            pltpu.VMEM((rows, LANES), F32),
            pltpu.VMEM((8 * LANES, LANES), F32),
            pltpu.VMEM((8 * LANES, LANES), F32),
            pltpu.SemaphoreType.DMA,
        ],
    )(recv, mid, z_low, z_high, x_low, x_high, weight)


def per_device(parcel_vel, parcel_props, fill_count, owner_peer, cell_offset, shell_weight, gas_state):
    _, nx, ny, nz = gas_state.shape
    blocks = parcel_vel.shape[0]
    send = call(pack_kernel, arr(blocks * ROWS, LANES))(
        owner_peer.reshape(1, blocks),
        cell_offset.reshape(1, blocks),
        fill_count.reshape(1, blocks),
        parcel_vel.transpose(1, 0, 2),
        parcel_props,
    )
    y_low, y_high = shift_pair(gas_state[:, :, :2], gas_state[:, :, ny - 2 :], "gy")
    whole = pl.BlockSpec(memory_space=pltpu.VMEM)
    where = pl.BlockSpec(memory_space=pl.ANY)
    mid, send = call(
        turn_kernel,
        [arr(nx, nz, LANES), arr(blocks * ROWS, LANES)],
        [pltpu.VMEM((nx, LANES, nz), F32)],
        in_specs=[whole, whole, whole, where],
        out_specs=[whole, where],
        input_output_aliases={3: 1},
    )(gas_state, y_low, y_high, send)
    recv = lax.all_to_all(
        send.reshape(blocks, ROWS * LANES), ("gx", "gy"), split_axis=0, concat_axis=0, tiled=True
    ).reshape(blocks * ROWS, LANES)
    z_low, z_high = shift_pair(mid[:, :2], mid[:, nz - 2 :], "gz")

    def face(lo, hi):
        zero = jnp.zeros((2, ZO - 2, LANES), F32)
        return jnp.concatenate([zero, z_low[lo:hi], mid[lo:hi], z_high[lo:hi], zero], axis=1)

    x_low, x_high = shift_pair(face(0, 2), face(nx - 2, nx), "gx")
    halo = (mid, z_low, z_high, x_low, x_high)

    weight = shell_weight.reshape(LANES, 4, 4, 8).transpose(2, 1, 3, 0).reshape(LANES, LANES)
    pay, total, x_lo, x_hi = parcels(recv, *halo, weight)
    parcels_next = pay.transpose(1, 0, 2)
    base = call(diffuse_kernel, arr(nx, nz, LANES), [pltpu.VMEM((2, ZR, LANES), F32)])(*halo)

    from_low, from_high = shift_pair(x_lo.reshape(2, ZR, LANES), x_hi.reshape(2, ZR, LANES), "gx")
    total = total.reshape(nx, ZR, LANES)

    def rim(lo, hi):
        part = total[:, lo:hi]
        return jnp.concatenate(
            [part[:2] + from_low[:, lo:hi], part[2 : nx - 2], part[nx - 2 :] + from_high[:, lo:hi]], axis=0
        )

    z_below, z_above = shift_pair(rim(ZO - 2, ZO), rim(ZO + nz, ZO + nz + 2), "gz")
    rows_out, y_lo, y_hi = call(
        back_kernel,
        [arr(4, nx, ny, nz), arr(4, nx, 2, nz), arr(4, nx, 2, nz)],
        [pltpu.VMEM((nx, nz, LANES), F32)],
    )(total, base, from_low, from_high, z_below, z_above)
    y_below, y_above = shift_pair(y_lo, y_hi, "gy")
    gas_next = jnp.concatenate(
        [rows_out[:, :, :2] + y_below, rows_out[:, :, 2 : ny - 2], rows_out[:, :, ny - 2 :] + y_above], axis=2
    )
    return parcels_next, gas_next


def solution(mesh):
    return jax.shard_map(
        per_device,
        mesh=mesh,
        in_specs=(
            P(("gx", "gy", "gz"), None, None),
            P(("gx", "gy", "gz"), None, None),
            P(("gx", "gy", "gz")),
            P(("gx", "gy", "gz"), None),
            P(("gx", "gy", "gz")),
            P(),
            P(None, "gx", "gy", "gz"),
        ),
        out_specs=(P(("gx", "gy", "gz"), None, None), P(None, "gx", "gy", "gz")),
        check_vma=False,
    )
```

```python
import functools
import jax
import jax.numpy as jnp
from jax import lax
from jax.experimental import pallas as pl
from jax.experimental.pallas import tpu as pltpu
from jax.sharding import PartitionSpec as P

TIME_STEP = 0.05
SETTLING = 1.0
F32 = jnp.float32
BF16 = jnp.bfloat16
HI = lax.Precision.HIGHEST

LANES = 128
NEARLY_ALL = 66200000
ROWS = 11
ZR = 144
ZO = 8
YS = 32


def iota(shape, dim):
    return lax.broadcasted_iota(jnp.int32, shape, dim)


def pack_kernel(tgt_hbm, off_hbm, cnt_hbm, vel_hbm, prop_hbm, out_ref, tgt_ref, off_ref, cnt_ref, vel_ref, prop_ref, sems):
    n = LANES
    pairs = ((tgt_hbm, tgt_ref), (off_hbm, off_ref), (cnt_hbm, cnt_ref), (vel_hbm, vel_ref), (prop_hbm, prop_ref))
    copies = [pltpu.make_async_copy(src, dst, sems.at[i]) for i, (src, dst) in enumerate(pairs)]
    for copy in copies:
        copy.start()
    for copy in copies:
        copy.wait()
    hot = (iota((n, n), 0) == tgt_ref[...]).astype(F32)
    earlier = (iota((n, n), 0) < iota((n, n), 1)).astype(BF16)
    rank = jnp.dot(hot.astype(BF16), earlier, preferred_element_type=F32)
    first = jnp.where(rank < 0.5, hot, 0.0)
    second = jnp.where(rank > 0.5, hot, 0.0)
    off = off_ref[...].astype(F32)
    cnt = cnt_ref[...].astype(F32)
    lane = iota((n, n), 1)
    head = jnp.zeros((n, n), F32)
    for place, (pick, val) in enumerate(((first, off), (second, off), (first, cnt), (second, cnt))):
        column = jnp.sum(pick * val, axis=1, keepdims=True)
        head = jnp.where(lane == place, column, head)
    out_ref[pl.ds(10, n, stride=ROWS), :] = head
    picks = jnp.concatenate([first, second], axis=0).astype(BF16)
    for k in range(5):
        x = vel_ref[k] if k < 3 else prop_ref[:, k - 3, :]
        total = jnp.zeros((2 * n, n), F32)
        for _ in range(3):
            part = x.astype(BF16)
            x = x - part.astype(F32)
            total = total + jnp.dot(picks, part, preferred_element_type=F32)
        out_ref[pl.ds(k, n, stride=ROWS), :] = total[:n]
        out_ref[pl.ds(5 + k, n, stride=ROWS), :] = total[n:]


def turn_kernel(gas_ref, xl_ref, xh_ref, yl_ref, yh_ref, out_ref, buf):
    cells_x, cells_y = gas_ref.shape[1], gas_ref.shape[2]
    buf[...] = jnp.zeros_like(buf)
    for x in range(cells_x + 4):
        ref, at = (xl_ref, x) if x < 2 else (gas_ref, x - 2) if x < cells_x + 2 else (xh_ref, x - cells_x - 2)
        for k in range(4):
            buf[x, k * YS : k * YS + 2, :] = yl_ref[k, x]
            buf[x, k * YS + 2 : k * YS + 2 + cells_y, :] = ref[k, at]
            buf[x, k * YS + 2 + cells_y : k * YS + 4 + cells_y, :] = yh_ref[k, x]
    for x in range(cells_x + 4):
        out_ref[x] = buf[x].T


def diffuse_kernel(mid_ref, zl_ref, zh_ref, out_ref, col):
    cells_x, cells_z = out_ref.shape[0], out_ref.shape[1]
    last = ZO + cells_z
    lane = iota((cells_z, LANES), 1)
    rate = jnp.where(lane < 3 * YS, TIME_STEP, 0.5 * TIME_STEP).astype(F32)
    for x in range(2, cells_x + 2):
        here = mid_ref[x]
        col[x % 2, ZO:last, :] = here
        col[x % 2, ZO - 2 : ZO, :] = zl_ref[x]
        col[x % 2, last : last + 2, :] = zh_ref[x]
        beside = mid_ref[x - 1] + mid_ref[x + 1] + pltpu.roll(here, LANES - 1, 1) + pltpu.roll(here, 1, 1)
        beside = beside + col[x % 2, ZO + 1 : last + 1, :] + col[x % 2, ZO - 1 : last - 1, :]
        out_ref[x - 2] = here + rate * (beside - 6.0 * here)


def parcel_kernel(
    recv_ref, mid_ref, zl_ref, zh_ref, w_ref,
    pay_ref, sum_ref, xlo_ref, xhi_ref,
    code_v, code_s, pad, acc, more, near, force, sem,
):
    planes, cells_z = mid_ref.shape[0], mid_ref.shape[1]
    last = ZO + cells_z
    n = LANES
    off = recv_ref[pl.ds(10, n, stride=ROWS), :]
    rest = jnp.floor((off + 0.5) * (1.0 / 125.0))
    oz = off - rest * 125.0
    ox = jnp.floor((rest + 0.5) * (1.0 / 17.0))
    oy = rest - ox * 17.0
    code = oy * 4096.0 + ox * float(ZR) + oz + float(ZO - 2)
    code_v[...] = code.T[0:8].astype(jnp.int32)
    copy = pltpu.make_async_copy(code_v, code_s, sem)
    copy.start()
    for x in range(planes):
        at = x * ZR
        pad[at + ZO : at + last, :] = mid_ref[x]
        pad[at + ZO - 2 : at + ZO, :] = zl_ref[x]
        pad[at + last : at + last + 2, :] = zh_ref[x]
    acc[...] = jnp.zeros_like(acc)
    more[...] = jnp.zeros_like(more)
    w_hi = w_ref[...].astype(BF16)
    w_lo = (w_ref[...] - w_hi.astype(F32)).astype(BF16)

    def split(x):
        hi = x.astype(BF16)
        return hi, (x - hi.astype(F32)).astype(BF16)

    copy.wait()

    lane8 = iota((8, n), 1)
    group = (lane8 % YS) // 4
    quad = lane8 % 4
    lane = iota((YS, n), 1)

    def place(s, b):
        c = code_s[s // 4, (s % 4) * YS + b]
        return jnp.bitwise_and(c, 4095), lax.shift_right_logical(c, 12)

    @pl.loop(0, 8)
    def _(s):
        merged = []
        for g in range(4):
            total = [None] * 4
            for b8 in range(8):
                at, oy_b = place(s, b8 * 4 + g)
                shift = jnp.bitwise_and(4 * b8 - oy_b, n - 1)
                mine = group == b8
                for a in range(4):
                    x = pltpu.roll(pad[pl.ds(at + a * ZR, 8), :], shift, 1)
                    total[a] = jnp.where(mine, x, 0.0 if total[a] is None else total[a])
            merged.append(total)
        cells = []
        for e in range(4):
            for a in range(4):
                x = merged[0][a]
                out = pltpu.roll(x, -e % n, 1) if e else x
                for g in range(1, 4):
                    x = merged[g][a]
                    x = pltpu.roll(x, (g - e) % n, 1) if g != e else x
                    out = jnp.where(quad == g, x, out)
                cells.append(out)
        near[pl.ds(pl.multiple_of(s * n, n), n), :] = jnp.concatenate(cells, axis=0).T

    near_hi, near_lo = split(near[...])
    gas_all = jnp.dot(
        jnp.concatenate([near_hi, near_lo], axis=1), jnp.concatenate([w_hi, w_hi], axis=0), preferred_element_type=F32
    ) + jnp.dot(near_hi, w_lo, preferred_element_type=F32)
    for s in range(8):
        rank, q0 = s // 4, (s % 4) * YS
        row = q0 * ROWS + rank * 5

        def take(k):
            return recv_ref[pl.ds(row + k, YS, stride=ROWS), :]

        head = recv_ref[pl.ds(q0 * ROWS + 10, YS, stride=ROWS), :]
        alive = lane.astype(F32) < head[:, 2 + rank : 3 + rank]
        mass = jnp.where(alive, take(3), 0.0)
        relax = jnp.where(alive, take(4), 1.0)
        drag = TIME_STEP / relax
        under = 1.0 / (1.0 + drag)
        slots = pl.ds(2 * q0 + rank, YS, stride=2)
        for k in range(3):
            gas = gas_all[s * n + k * YS : s * n + (k + 1) * YS]
            settle = TIME_STEP * SETTLING if k == 2 else 0.0
            vel = (take(k) + drag * gas - settle) * under
            force[s * n + k * YS : s * n + (k + 1) * YS, :] = -(mass * drag * (gas - vel))
            pay_ref[k, slots, :] = jnp.where(alive, vel, 0.0)
        pay_ref[3, slots, :] = mass
        pay_ref[4, slots, :] = jnp.where(alive, relax, 0.0)
        force[s * n + 3 * YS : (s + 1) * n, :] = mass
    across = (((1,), (1,)), ((), ()))
    for s in range(8):
        f_hi, f_lo = split(force[s * n : (s + 1) * n, :])
        near[s * n : (s + 1) * n, :] = lax.dot_general(
            jnp.concatenate([w_hi, w_lo], axis=1),
            jnp.concatenate([f_hi, f_hi], axis=1),
            across,
            preferred_element_type=F32,
        ) + lax.dot_general(w_hi, f_lo, across, preferred_element_type=F32)

    @pl.loop(0, 8)
    def _(s):
        spread = near[pl.ds(pl.multiple_of(s * n, n), n), :]
        for g in range(4):
            parts = []
            for a in range(4):
                out = None
                for e in range(4):
                    x = spread[(e * 4 + a) * 8 : (e * 4 + a) * 8 + 8]
                    x = pltpu.roll(x, (e - g) % n, 1) if e != g else x
                    out = x if out is None else jnp.where(quad == e, x, out)
                parts.append(out)
            for b8 in range(0, 8, 2):
                work = []
                for half, sums in enumerate((acc, more)):
                    at, oy_b = place(s, (b8 + half) * 4 + g)
                    shift = jnp.bitwise_and(oy_b - 4 * (b8 + half), n - 1)
                    mine = group == b8 + half
                    for a in range(4):
                        add = pltpu.roll(jnp.where(mine, parts[a], 0.0), shift, 1)
                        work.append((sums, pl.ds(at + a * ZR, 8), add))
                olds = [sums[rows, :] for sums, rows, _ in work]
                for (sums, rows, add), old in zip(work, olds):
                    sums[rows, :] = old + add

    low, high = 2 * ZR, (planes - 2) * ZR
    sum_ref[...] = acc[low:high, :] + more[low:high, :]
    xlo_ref[...] = acc[0:low, :] + more[0:low, :]
    xhi_ref[...] = acc[high:, :] + more[high:, :]


def back_kernel(sum_ref, base_ref, xl_ref, xh_ref, zl_ref, zh_ref, out_ref, ylo_ref, yhi_ref, buf):
    cells_x = sum_ref.shape[0]
    cells_z = out_ref.shape[3]
    cells_y = out_ref.shape[2]
    for x in range(cells_x):
        value = sum_ref[x, ZO : ZO + cells_z, :]
        if x < 2:
            value = value + xl_ref[x, ZO : ZO + cells_z, :]
        if x >= cells_x - 2:
            value = value + xh_ref[x - cells_x + 2, ZO : ZO + cells_z, :]
        buf[x] = value
    buf[:, 0:2, :] += zl_ref[...]
    buf[:, cells_z - 2 : cells_z, :] += zh_ref[...]
    lane = iota((cells_z, LANES), 1)
    inside = (lane % YS >= 2) & (lane % YS < 2 + cells_y)
    for x in range(cells_x):
        flat = (buf[x] + jnp.where(inside, base_ref[x], 0.0)).T
        for k in range(4):
            out_ref[k, x] = flat[k * YS + 2 : k * YS + 2 + cells_y]
            ylo_ref[k, x] = flat[k * YS : k * YS + 2]
            yhi_ref[k, x] = flat[k * YS + 2 + cells_y : k * YS + 4 + cells_y]


def shift_pair(to_low, to_high, axis, ring=False):
    count = lax.axis_size(axis)
    if not ring:
        up = [(i, i + 1) for i in range(count - 1)]
        down = [(j, i) for i, j in up]
        return lax.ppermute(to_high, axis, up), lax.ppermute(to_low, axis, down)
    up = [(i, (i + 1) % count) for i in range(count)]
    down = [(j, i) for i, j in up]
    here = lax.axis_index(axis)
    low, high = lax.ppermute(to_high, axis, up), lax.ppermute(to_low, axis, down)
    return jnp.where(here > 0, low, 0.0), jnp.where(here < count - 1, high, 0.0)


def call(kernel, outs, scratch=(), vmem=40 * 2**20, **kw):
    return pl.pallas_call(
        kernel,
        out_shape=outs,
        scratch_shapes=list(scratch),
        compiler_params=pltpu.CompilerParams(vmem_limit_bytes=vmem),
        **kw,
    )


def arr(*shape, dtype=F32):
    return jax.ShapeDtypeStruct(shape, dtype)


def parcels(recv, mid, z_low, z_high, weight):
    nx = mid.shape[0] - 4
    blocks = recv.shape[0] // ROWS
    rows = (nx + 4) * ZR
    return call(
        parcel_kernel,
        [arr(5, 2 * blocks, LANES), arr(nx * ZR, LANES), arr(2 * ZR, LANES), arr(2 * ZR, LANES)],
        [
            pltpu.VMEM((8, LANES), jnp.int32),
            pltpu.SMEM((8, LANES), jnp.int32),
            pltpu.VMEM((rows, LANES), F32),
            pltpu.VMEM((rows, LANES), F32),
            pltpu.VMEM((rows, LANES), F32),
            pltpu.VMEM((8 * LANES, LANES), F32),
            pltpu.VMEM((8 * LANES, LANES), F32),
            pltpu.SemaphoreType.DMA,
        ],
    )(recv, mid, z_low, z_high, weight)


def per_device(parcel_vel, parcel_props, fill_count, owner_peer, cell_offset, shell_weight, gas_state):
    _, nx, ny, nz = gas_state.shape
    blocks = parcel_vel.shape[0]
    x_low, x_high = shift_pair(gas_state[:, :2], gas_state[:, nx - 2 :], "gx", ring=True)
    send = call(
        pack_kernel,
        arr(blocks * ROWS, LANES),
        [pltpu.VMEM((1, blocks), jnp.int32)] * 3
        + [
            pltpu.VMEM((3, blocks, LANES), F32),
            pltpu.VMEM((blocks, 2, LANES), F32),
            pltpu.SemaphoreType.DMA((5,)),
        ],
        in_specs=[pl.BlockSpec(memory_space=pltpu.HBM)] * 5,
        vmem=NEARLY_ALL,
    )(
        owner_peer.reshape(1, blocks),
        cell_offset.reshape(1, blocks),
        fill_count.reshape(1, blocks),
        parcel_vel.transpose(1, 0, 2),
        parcel_props,
    )
    send, x_low, x_high = lax.optimization_barrier((send, x_low, x_high))

    def y_face(lo):
        return jnp.concatenate([x_low[:, :, lo : lo + 2], gas_state[:, :, lo : lo + 2], x_high[:, :, lo : lo + 2]], axis=1)

    y_lo, y_hi = y_face(0), y_face(ny - 2)
    recv = lax.all_to_all(
        send.reshape(blocks, ROWS * LANES), ("gx", "gy"), split_axis=0, concat_axis=0, tiled=True
    ).reshape(blocks * ROWS, LANES)
    y_low, y_high = shift_pair(y_lo, y_hi, "gy")
    mid = call(turn_kernel, arr(nx + 4, nz, LANES), [pltpu.VMEM((nx + 4, LANES, nz), F32)])(
        gas_state, x_low, x_high, y_low, y_high
    )
    halo = (mid, *shift_pair(mid[:, :2], mid[:, nz - 2 :], "gz"))

    weight = shell_weight.reshape(LANES, 4, 4, 8).transpose(2, 1, 3, 0).reshape(LANES, LANES)
    pay, total, x_lo, x_hi = parcels(recv, *halo, weight)
    parcels_next = pay.transpose(1, 0, 2)
    base = call(diffuse_kernel, arr(nx, nz, LANES), [pltpu.VMEM((2, ZR, LANES), F32)])(*halo)

    from_low, from_high = shift_pair(x_lo.reshape(2, ZR, LANES), x_hi.reshape(2, ZR, LANES), "gx", ring=True)
    total = total.reshape(nx, ZR, LANES)

    def rim(lo, hi):
        part = total[:, lo:hi]
        return jnp.concatenate(
            [part[:2] + from_low[:, lo:hi], part[2 : nx - 2], part[nx - 2 :] + from_high[:, lo:hi]], axis=0
        )

    z_below, z_above = shift_pair(rim(ZO - 2, ZO), rim(ZO + nz, ZO + nz + 2), "gz")
    rows_out, y_lo, y_hi = call(
        back_kernel,
        [arr(4, nx, ny, nz), arr(4, nx, 2, nz), arr(4, nx, 2, nz)],
        [pltpu.VMEM((nx, nz, LANES), F32)],
    )(total, base, from_low, from_high, z_below, z_above)
    y_below, y_above = shift_pair(y_lo, y_hi, "gy")
    gas_next = jnp.concatenate(
        [rows_out[:, :, :2] + y_below, rows_out[:, :, 2 : ny - 2], rows_out[:, :, ny - 2 :] + y_above], axis=2
    )
    return parcels_next, gas_next


def solution(mesh):
    return jax.shard_map(
        per_device,
        mesh=mesh,
        in_specs=(
            P(("gx", "gy", "gz"), None, None),
            P(("gx", "gy", "gz"), None, None),
            P(("gx", "gy", "gz")),
            P(("gx", "gy", "gz"), None),
            P(("gx", "gy", "gz")),
            P(),
            P(None, "gx", "gy", "gz"),
        ),
        out_specs=(P(("gx", "gy", "gz"), None, None), P(None, "gx", "gy", "gz")),
        check_vma=False,
    )
```

```python
import functools
import jax
import jax.numpy as jnp
from jax import lax
from jax.experimental import pallas as pl
from jax.experimental.pallas import tpu as pltpu
from jax.sharding import PartitionSpec as P

TIME_STEP = 0.05
SETTLING = 1.0
F32 = jnp.float32
BF16 = jnp.bfloat16
HI = lax.Precision.HIGHEST

LANES = 128
NEARLY_ALL = 66200000
ROWS = 11
ZR = 144
ZO = 8
YS = 32


def iota(shape, dim):
    return lax.broadcasted_iota(jnp.int32, shape, dim)


def pack_kernel(tgt_hbm, off_hbm, cnt_hbm, vel_hbm, prop_hbm, out_ref, tgt_ref, off_ref, cnt_ref, vel_ref, prop_ref, sems):
    n = LANES
    pairs = ((tgt_hbm, tgt_ref), (off_hbm, off_ref), (cnt_hbm, cnt_ref), (vel_hbm, vel_ref), (prop_hbm, prop_ref))
    copies = [pltpu.make_async_copy(src, dst, sems.at[i]) for i, (src, dst) in enumerate(pairs)]
    for copy in copies:
        copy.start()
    for copy in copies:
        copy.wait()
    hot = (iota((n, n), 0) == tgt_ref[...]).astype(F32)
    earlier = (iota((n, n), 0) < iota((n, n), 1)).astype(BF16)
    rank = jnp.dot(hot.astype(BF16), earlier, preferred_element_type=F32)
    first = jnp.where(rank < 0.5, hot, 0.0)
    second = jnp.where(rank > 0.5, hot, 0.0)
    off = off_ref[...].astype(F32)
    cnt = cnt_ref[...].astype(F32)
    lane = iota((n, n), 1)
    head = jnp.zeros((n, n), F32)
    for place, (pick, val) in enumerate(((first, off), (second, off), (first, cnt), (second, cnt))):
        column = jnp.sum(pick * val, axis=1, keepdims=True)
        head = jnp.where(lane == place, column, head)
    out_ref[pl.ds(10, n, stride=ROWS), :] = head
    picks = jnp.concatenate([first, second], axis=0).astype(BF16)
    for k in range(5):
        x = vel_ref[k] if k < 3 else prop_ref[:, k - 3, :]
        total = jnp.zeros((2 * n, n), F32)
        for _ in range(3):
            part = x.astype(BF16)
            x = x - part.astype(F32)
            total = total + jnp.dot(picks, part, preferred_element_type=F32)
        out_ref[pl.ds(k, n, stride=ROWS), :] = total[:n]
        out_ref[pl.ds(5 + k, n, stride=ROWS), :] = total[n:]


def fill_rows(buf, gas_ref, xl_ref, xh_ref):
    cells_x, cells_y = gas_ref.shape[1], gas_ref.shape[2]
    for x in range(cells_x + 4):
        ref, at = (xl_ref, x) if x < 2 else (gas_ref, x - 2) if x < cells_x + 2 else (xh_ref, x - cells_x - 2)
        for k in range(4):
            buf[x, k * YS + 2 : k * YS + 2 + cells_y, :] = ref[k, at]


def edge_kernel(gas_ref, xl_ref, xh_ref, lo_ref, hi_ref, buf):
    cells_z = gas_ref.shape[3]
    buf[...] = jnp.zeros_like(buf)
    fill_rows(buf, gas_ref, xl_ref, xh_ref)
    for x in range(lo_ref.shape[0]):
        flat = buf[x].T
        lo_ref[x] = flat[0:2]
        hi_ref[x] = flat[cells_z - 2 : cells_z]


def turn_kernel(gas_ref, xl_ref, xh_ref, zl_ref, zh_ref, yl_ref, yh_ref, out_ref, zlo_ref, zhi_ref, buf):
    planes, cells_y = out_ref.shape[0], gas_ref.shape[2]
    buf[...] = jnp.zeros_like(buf)
    fill_rows(buf, gas_ref, xl_ref, xh_ref)
    y = iota((2, LANES), 1) % YS
    for x in range(planes):
        for k in range(4):
            row = (k * planes + x) * 2
            buf[x, k * YS : k * YS + 2, :] = yl_ref[row : row + 2]
            buf[x, k * YS + 2 + cells_y : k * YS + 4 + cells_y, :] = yh_ref[row : row + 2]
        for part, (z_ref, o_ref) in enumerate(((zl_ref, zlo_ref), (zh_ref, zhi_ref))):
            row = (4 + part) * planes * 2 + x * 2
            below = pltpu.roll(yl_ref[row : row + 2], LANES - cells_y, 1)
            above = pltpu.roll(yh_ref[row : row + 2], cells_y, 1)
            o_ref[x] = jnp.where(y < 2, below, jnp.where(y < 2 + cells_y, z_ref[x], jnp.where(y < 4 + cells_y, above, 0.0)))
    for x in range(planes):
        out_ref[x] = buf[x].T


def diffuse_kernel(mid_ref, zl_ref, zh_ref, out_ref, col):
    cells_x, cells_z = out_ref.shape[0], out_ref.shape[1]
    last = ZO + cells_z
    lane = iota((cells_z, LANES), 1)
    rate = jnp.where(lane < 3 * YS, TIME_STEP, 0.5 * TIME_STEP).astype(F32)
    for x in range(2, cells_x + 2):
        here = mid_ref[x]
        col[x % 2, ZO:last, :] = here
        col[x % 2, ZO - 2 : ZO, :] = zl_ref[x]
        col[x % 2, last : last + 2, :] = zh_ref[x]
        beside = mid_ref[x - 1] + mid_ref[x + 1] + pltpu.roll(here, LANES - 1, 1) + pltpu.roll(here, 1, 1)
        beside = beside + col[x % 2, ZO + 1 : last + 1, :] + col[x % 2, ZO - 1 : last - 1, :]
        out_ref[x - 2] = here + rate * (beside - 6.0 * here)


def parcel_kernel(
    recv_ref, mid_ref, zl_ref, zh_ref, w_ref,
    pay_ref, sum_ref, xlo_ref, xhi_ref,
    code_v, code_s, pad, acc, more, near, force, sem,
):
    planes, cells_z = mid_ref.shape[0], mid_ref.shape[1]
    last = ZO + cells_z
    n = LANES
    off = recv_ref[pl.ds(10, n, stride=ROWS), :]
    rest = jnp.floor((off + 0.5) * (1.0 / 125.0))
    oz = off - rest * 125.0
    ox = jnp.floor((rest + 0.5) * (1.0 / 17.0))
    oy = rest - ox * 17.0
    code = oy * 4096.0 + ox * float(ZR) + oz + float(ZO - 2)
    code_v[...] = code.T[0:8].astype(jnp.int32)
    copy = pltpu.make_async_copy(code_v, code_s, sem)
    copy.start()
    for x in range(planes):
        at = x * ZR
        pad[at + ZO : at + last, :] = mid_ref[x]
        pad[at + ZO - 2 : at + ZO, :] = zl_ref[x]
        pad[at + last : at + last + 2, :] = zh_ref[x]
    acc[...] = jnp.zeros_like(acc)
    more[...] = jnp.zeros_like(more)
    w_hi = w_ref[...].astype(BF16)
    w_lo = (w_ref[...] - w_hi.astype(F32)).astype(BF16)

    def split(x):
        hi = x.astype(BF16)
        return hi, (x - hi.astype(F32)).astype(BF16)

    copy.wait()

    lane8 = iota((8, n), 1)
    group = (lane8 % YS) // 4
    quad = lane8 % 4
    lane = iota((YS, n), 1)

    def place(s, b):
        c = code_s[s // 4, (s % 4) * YS + b]
        return jnp.bitwise_and(c, 4095), lax.shift_right_logical(c, 12)

    @pl.loop(0, 8)
    def _(s):
        merged = []
        for g in range(4):
            total = [None] * 4
            for b8 in range(8):
                at, oy_b = place(s, b8 * 4 + g)
                shift = jnp.bitwise_and(4 * b8 - oy_b, n - 1)
                mine = group == b8
                for a in range(4):
                    x = pltpu.roll(pad[pl.ds(at + a * ZR, 8), :], shift, 1)
                    total[a] = jnp.where(mine, x, 0.0 if total[a] is None else total[a])
            merged.append(total)
        cells = []
        for e in range(4):
            for a in range(4):
                x = merged[0][a]
                out = pltpu.roll(x, -e % n, 1) if e else x
                for g in range(1, 4):
                    x = merged[g][a]
                    x = pltpu.roll(x, (g - e) % n, 1) if g != e else x
                    out = jnp.where(quad == g, x, out)
                cells.append(out)
        near[pl.ds(pl.multiple_of(s * n, n), n), :] = jnp.concatenate(cells, axis=0).T

    near_hi, near_lo = split(near[...])
    gas_all = jnp.dot(
        jnp.concatenate([near_hi, near_lo], axis=1), jnp.concatenate([w_hi, w_hi], axis=0), preferred_element_type=F32
    ) + jnp.dot(near_hi, w_lo, preferred_element_type=F32)
    for s in range(8):
        rank, q0 = s // 4, (s % 4) * YS
        row = q0 * ROWS + rank * 5

        def take(k):
            return recv_ref[pl.ds(row + k, YS, stride=ROWS), :]

        head = recv_ref[pl.ds(q0 * ROWS + 10, YS, stride=ROWS), :]
        alive = lane.astype(F32) < head[:, 2 + rank : 3 + rank]
        mass = jnp.where(alive, take(3), 0.0)
        relax = jnp.where(alive, take(4), 1.0)
        drag = TIME_STEP / relax
        under = 1.0 / (1.0 + drag)
        slots = pl.ds(2 * q0 + rank, YS, stride=2)
        for k in range(3):
            gas = gas_all[s * n + k * YS : s * n + (k + 1) * YS]
            settle = TIME_STEP * SETTLING if k == 2 else 0.0
            vel = (take(k) + drag * gas - settle) * under
            force[s * n + k * YS : s * n + (k + 1) * YS, :] = -(mass * drag * (gas - vel))
            pay_ref[k, slots, :] = jnp.where(alive, vel, 0.0)
        pay_ref[3, slots, :] = mass
        pay_ref[4, slots, :] = jnp.where(alive, relax, 0.0)
        force[s * n + 3 * YS : (s + 1) * n, :] = mass
    across = (((1,), (1,)), ((), ()))
    for s in range(8):
        f_hi, f_lo = split(force[s * n : (s + 1) * n, :])
        near[s * n : (s + 1) * n, :] = lax.dot_general(
            jnp.concatenate([w_hi, w_lo], axis=1),
            jnp.concatenate([f_hi, f_hi], axis=1),
            across,
            preferred_element_type=F32,
        ) + lax.dot_general(w_hi, f_lo, across, preferred_element_type=F32)

    @pl.loop(0, 8)
    def _(s):
        spread = near[pl.ds(pl.multiple_of(s * n, n), n), :]
        for g in range(4):
            parts = []
            for a in range(4):
                out = None
                for e in range(4):
                    x = spread[(e * 4 + a) * 8 : (e * 4 + a) * 8 + 8]
                    x = pltpu.roll(x, (e - g) % n, 1) if e != g else x
                    out = x if out is None else jnp.where(quad == e, x, out)
                parts.append(out)
            for b8 in range(0, 8, 2):
                work = []
                for half, sums in enumerate((acc, more)):
                    at, oy_b = place(s, (b8 + half) * 4 + g)
                    shift = jnp.bitwise_and(oy_b - 4 * (b8 + half), n - 1)
                    mine = group == b8 + half
                    for a in range(4):
                        add = pltpu.roll(jnp.where(mine, parts[a], 0.0), shift, 1)
                        work.append((sums, pl.ds(at + a * ZR, 8), add))
                olds = [sums[rows, :] for sums, rows, _ in work]
                for (sums, rows, add), old in zip(work, olds):
                    sums[rows, :] = old + add

    low, high = 2 * ZR, (planes - 2) * ZR
    sum_ref[...] = acc[low:high, :] + more[low:high, :]
    xlo_ref[...] = acc[0:low, :] + more[0:low, :]
    xhi_ref[...] = acc[high:, :] + more[high:, :]


def back_kernel(sum_ref, base_ref, xl_ref, xh_ref, zl_ref, zh_ref, out_ref, ylo_ref, yhi_ref, buf):
    cells_x = sum_ref.shape[0]
    cells_z = out_ref.shape[3]
    cells_y = out_ref.shape[2]
    for x in range(cells_x):
        value = sum_ref[x, ZO : ZO + cells_z, :]
        if x < 2:
            value = value + xl_ref[x, ZO : ZO + cells_z, :]
        if x >= cells_x - 2:
            value = value + xh_ref[x - cells_x + 2, ZO : ZO + cells_z, :]
        buf[x] = value
    buf[:, 0:2, :] += zl_ref[...]
    buf[:, cells_z - 2 : cells_z, :] += zh_ref[...]
    lane = iota((cells_z, LANES), 1)
    inside = (lane % YS >= 2) & (lane % YS < 2 + cells_y)
    for x in range(cells_x):
        flat = (buf[x] + jnp.where(inside, base_ref[x], 0.0)).T
        for k in range(4):
            out_ref[k, x] = flat[k * YS + 2 : k * YS + 2 + cells_y]
            ylo_ref[k, x] = flat[k * YS : k * YS + 2]
            yhi_ref[k, x] = flat[k * YS + 2 + cells_y : k * YS + 4 + cells_y]


def shift_pair(to_low, to_high, axis, ring=False):
    count = lax.axis_size(axis)
    if not ring:
        up = [(i, i + 1) for i in range(count - 1)]
        down = [(j, i) for i, j in up]
        return lax.ppermute(to_high, axis, up), lax.ppermute(to_low, axis, down)
    up = [(i, (i + 1) % count) for i in range(count)]
    down = [(j, i) for i, j in up]
    here = lax.axis_index(axis)
    low, high = lax.ppermute(to_high, axis, up), lax.ppermute(to_low, axis, down)
    return jnp.where(here > 0, low, 0.0), jnp.where(here < count - 1, high, 0.0)


def call(kernel, outs, scratch=(), vmem=40 * 2**20, **kw):
    return pl.pallas_call(
        kernel,
        out_shape=outs,
        scratch_shapes=list(scratch),
        compiler_params=pltpu.CompilerParams(vmem_limit_bytes=vmem),
        **kw,
    )


def arr(*shape, dtype=F32):
    return jax.ShapeDtypeStruct(shape, dtype)


def parcels(recv, mid, z_low, z_high, weight):
    nx = mid.shape[0] - 4
    blocks = recv.shape[0] // ROWS
    rows = (nx + 4) * ZR
    return call(
        parcel_kernel,
        [arr(5, 2 * blocks, LANES), arr(nx * ZR, LANES), arr(2 * ZR, LANES), arr(2 * ZR, LANES)],
        [
            pltpu.VMEM((8, LANES), jnp.int32),
            pltpu.SMEM((8, LANES), jnp.int32),
            pltpu.VMEM((rows, LANES), F32),
            pltpu.VMEM((rows, LANES), F32),
            pltpu.VMEM((rows, LANES), F32),
            pltpu.VMEM((8 * LANES, LANES), F32),
            pltpu.VMEM((8 * LANES, LANES), F32),
            pltpu.SemaphoreType.DMA,
        ],
    )(recv, mid, z_low, z_high, weight)


def per_device(parcel_vel, parcel_props, fill_count, owner_peer, cell_offset, shell_weight, gas_state):
    _, nx, ny, nz = gas_state.shape
    blocks = parcel_vel.shape[0]
    x_low, x_high = shift_pair(gas_state[:, :2], gas_state[:, nx - 2 :], "gx", ring=True)
    send = call(
        pack_kernel,
        arr(blocks * ROWS, LANES),
        [pltpu.VMEM((1, blocks), jnp.int32)] * 3
        + [
            pltpu.VMEM((3, blocks, LANES), F32),
            pltpu.VMEM((blocks, 2, LANES), F32),
            pltpu.SemaphoreType.DMA((5,)),
        ],
        in_specs=[pl.BlockSpec(memory_space=pltpu.HBM)] * 5,
        vmem=NEARLY_ALL,
    )(
        owner_peer.reshape(1, blocks),
        cell_offset.reshape(1, blocks),
        fill_count.reshape(1, blocks),
        parcel_vel.transpose(1, 0, 2),
        parcel_props,
    )
    send, x_low, x_high = lax.optimization_barrier((send, x_low, x_high))
    recv = lax.all_to_all(
        send.reshape(blocks, ROWS * LANES), ("gx", "gy"), split_axis=0, concat_axis=0, tiled=True
    ).reshape(blocks * ROWS, LANES)
    planes = nx + 4
    rows_buf = [pltpu.VMEM((planes, LANES, nz), F32)]
    z_lo, z_hi = call(edge_kernel, [arr(planes, 2, LANES)] * 2, rows_buf)(gas_state, x_low, x_high)
    z_low, z_high = shift_pair(z_lo, z_hi, "gz")

    def y_face(lo):
        parts = [part[:, :, lo : lo + 2] for part in (x_low, gas_state, x_high)]
        face = jnp.concatenate(parts, axis=1).reshape(8 * planes, nz)
        return jnp.concatenate([face, z_low.reshape(2 * planes, LANES), z_high.reshape(2 * planes, LANES)], axis=0)

    y_low, y_high = shift_pair(y_face(0), y_face(ny - 2), "gy")
    halo = call(turn_kernel, [arr(planes, nz, LANES), arr(planes, 2, LANES), arr(planes, 2, LANES)], rows_buf)(
        gas_state, x_low, x_high, z_low, z_high, y_low, y_high
    )

    weight = shell_weight.reshape(LANES, 4, 4, 8).transpose(2, 1, 3, 0).reshape(LANES, LANES)
    pay, total, x_lo, x_hi = parcels(recv, *halo, weight)
    parcels_next = pay.transpose(1, 0, 2)
    base = call(diffuse_kernel, arr(nx, nz, LANES), [pltpu.VMEM((2, ZR, LANES), F32)])(*halo)

    from_low, from_high = shift_pair(x_lo.reshape(2, ZR, LANES), x_hi.reshape(2, ZR, LANES), "gx", ring=True)
    total = total.reshape(nx, ZR, LANES)

    def rim(lo, hi):
        part = total[:, lo:hi]
        return jnp.concatenate(
            [part[:2] + from_low[:, lo:hi], part[2 : nx - 2], part[nx - 2 :] + from_high[:, lo:hi]], axis=0
        )

    z_below, z_above = shift_pair(rim(ZO - 2, ZO), rim(ZO + nz, ZO + nz + 2), "gz")
    rows_out, y_lo, y_hi = call(
        back_kernel,
        [arr(4, nx, ny, nz), arr(4, nx, 2, nz), arr(4, nx, 2, nz)],
        [pltpu.VMEM((nx, nz, LANES), F32)],
    )(total, base, from_low, from_high, z_below, z_above)
    y_below, y_above = shift_pair(y_lo, y_hi, "gy")
    gas_next = jnp.concatenate(
        [rows_out[:, :, :2] + y_below, rows_out[:, :, 2 : ny - 2], rows_out[:, :, ny - 2 :] + y_above], axis=2
    )
    return parcels_next, gas_next


def solution(mesh):
    return jax.shard_map(
        per_device,
        mesh=mesh,
        in_specs=(
            P(("gx", "gy", "gz"), None, None),
            P(("gx", "gy", "gz"), None, None),
            P(("gx", "gy", "gz")),
            P(("gx", "gy", "gz"), None),
            P(("gx", "gy", "gz")),
            P(),
            P(None, "gx", "gy", "gz"),
        ),
        out_specs=(P(("gx", "gy", "gz"), None, None), P(None, "gx", "gy", "gz")),
        check_vma=False,
    )
```

```python
import functools
import jax
import jax.numpy as jnp
from jax import lax
from jax.experimental import pallas as pl
from jax.experimental.pallas import tpu as pltpu
from jax.sharding import PartitionSpec as P

TIME_STEP = 0.05
SETTLING = 1.0
F32 = jnp.float32
BF16 = jnp.bfloat16
HI = lax.Precision.HIGHEST

LANES = 128
NEARLY_ALL = 66200000
ROWS = 11
ZR = 144
ZO = 8
YS = 32


def iota(shape, dim):
    return lax.broadcasted_iota(jnp.int32, shape, dim)


def pack_kernel(tgt_hbm, off_hbm, cnt_hbm, vel_hbm, prop_hbm, out_ref, tgt_ref, off_ref, cnt_ref, vel_ref, prop_ref, sems):
    n = LANES
    pairs = ((tgt_hbm, tgt_ref), (off_hbm, off_ref), (cnt_hbm, cnt_ref), (vel_hbm, vel_ref), (prop_hbm, prop_ref))
    copies = [pltpu.make_async_copy(src, dst, sems.at[i]) for i, (src, dst) in enumerate(pairs)]
    for copy in copies:
        copy.start()
    for copy in copies:
        copy.wait()
    hot = (iota((n, n), 0) == tgt_ref[...]).astype(F32)
    earlier = (iota((n, n), 0) < iota((n, n), 1)).astype(BF16)
    rank = jnp.dot(hot.astype(BF16), earlier, preferred_element_type=F32)
    first = jnp.where(rank < 0.5, hot, 0.0)
    second = jnp.where(rank > 0.5, hot, 0.0)
    off = off_ref[...].astype(F32)
    cnt = cnt_ref[...].astype(F32)
    lane = iota((n, n), 1)
    head = jnp.zeros((n, n), F32)
    for place, (pick, val) in enumerate(((first, off), (second, off), (first, cnt), (second, cnt))):
        column = jnp.sum(pick * val, axis=1, keepdims=True)
        head = jnp.where(lane == place, column, head)
    out_ref[pl.ds(10, n, stride=ROWS), :] = head
    picks = jnp.concatenate([first, second], axis=0).astype(BF16)
    for k in range(5):
        x = vel_ref[k] if k < 3 else prop_ref[:, k - 3, :]
        total = jnp.zeros((2 * n, n), F32)
        for _ in range(3):
            part = x.astype(BF16)
            x = x - part.astype(F32)
            total = total + jnp.dot(picks, part, preferred_element_type=F32)
        out_ref[pl.ds(k, n, stride=ROWS), :] = total[:n]
        out_ref[pl.ds(5 + k, n, stride=ROWS), :] = total[n:]


def fill_rows(buf, gas_ref, xl_ref, xh_ref):
    cells_x, cells_y = gas_ref.shape[1], gas_ref.shape[2]
    for x in range(cells_x + 4):
        ref, at = (xl_ref, x) if x < 2 else (gas_ref, x - 2) if x < cells_x + 2 else (xh_ref, x - cells_x - 2)
        for k in range(4):
            buf[x, k * YS + 2 : k * YS + 2 + cells_y, :] = ref[k, at]


def edge_kernel(gas_ref, xl_ref, xh_ref, lo_ref, hi_ref, buf):
    cells_z = gas_ref.shape[3]
    buf[...] = jnp.zeros_like(buf)
    fill_rows(buf, gas_ref, xl_ref, xh_ref)
    for x in range(lo_ref.shape[0]):
        flat = buf[x].T
        lo_ref[x] = flat[0:2]
        hi_ref[x] = flat[cells_z - 2 : cells_z]


def turn_kernel(gas_ref, xl_ref, xh_ref, zl_ref, zh_ref, yl_ref, yh_ref, out_ref, zlo_ref, zhi_ref, buf):
    planes, cells_y = out_ref.shape[0], gas_ref.shape[2]
    buf[...] = jnp.zeros_like(buf)
    fill_rows(buf, gas_ref, xl_ref, xh_ref)
    y = iota((2, LANES), 1) % YS
    for x in range(planes):
        for k in range(4):
            row = (k * planes + x) * 2
            buf[x, k * YS : k * YS + 2, :] = yl_ref[row : row + 2]
            buf[x, k * YS + 2 + cells_y : k * YS + 4 + cells_y, :] = yh_ref[row : row + 2]
        for part, (z_ref, o_ref) in enumerate(((zl_ref, zlo_ref), (zh_ref, zhi_ref))):
            row = (4 + part) * planes * 2 + x * 2
            below = pltpu.roll(yl_ref[row : row + 2], LANES - cells_y, 1)
            above = pltpu.roll(yh_ref[row : row + 2], cells_y, 1)
            o_ref[x] = jnp.where(y < 2, below, jnp.where(y < 2 + cells_y, z_ref[x], jnp.where(y < 4 + cells_y, above, 0.0)))
    for x in range(planes):
        out_ref[x] = buf[x].T


def diffuse_kernel(mid_ref, zl_ref, zh_ref, out_ref, col):
    cells_x, cells_z = out_ref.shape[0], out_ref.shape[1]
    last = ZO + cells_z
    lane = iota((cells_z, LANES), 1)
    rate = jnp.where(lane < 3 * YS, TIME_STEP, 0.5 * TIME_STEP).astype(F32)
    for x in range(2, cells_x + 2):
        here = mid_ref[x]
        col[x % 2, ZO:last, :] = here
        col[x % 2, ZO - 2 : ZO, :] = zl_ref[x]
        col[x % 2, last : last + 2, :] = zh_ref[x]
        beside = mid_ref[x - 1] + mid_ref[x + 1] + pltpu.roll(here, LANES - 1, 1) + pltpu.roll(here, 1, 1)
        beside = beside + col[x % 2, ZO + 1 : last + 1, :] + col[x % 2, ZO - 1 : last - 1, :]
        out_ref[x - 2] = here + rate * (beside - 6.0 * here)


def parcel_kernel(
    recv_ref, mid_ref, zl_ref, zh_ref, w_ref,
    pay_hbm, sum_ref, xlo_ref, xhi_ref,
    code_v, code_s, pad, acc, more, near, force, pay_ref, sem, pay_sem,
):
    planes, cells_z = mid_ref.shape[0], mid_ref.shape[1]
    last = ZO + cells_z
    n = LANES
    off = recv_ref[pl.ds(10, n, stride=ROWS), :]
    rest = jnp.floor((off + 0.5) * (1.0 / 125.0))
    oz = off - rest * 125.0
    ox = jnp.floor((rest + 0.5) * (1.0 / 17.0))
    oy = rest - ox * 17.0
    code = oy * 4096.0 + ox * float(ZR) + oz + float(ZO - 2)
    code_v[...] = code.T[0:8].astype(jnp.int32)
    copy = pltpu.make_async_copy(code_v, code_s, sem)
    copy.start()
    for x in range(planes):
        at = x * ZR
        pad[at + ZO : at + last, :] = mid_ref[x]
        pad[at + ZO - 2 : at + ZO, :] = zl_ref[x]
        pad[at + last : at + last + 2, :] = zh_ref[x]
    acc[...] = jnp.zeros_like(acc)
    more[...] = jnp.zeros_like(more)
    w_hi = w_ref[...].astype(BF16)
    w_lo = (w_ref[...] - w_hi.astype(F32)).astype(BF16)

    def split(x):
        hi = x.astype(BF16)
        return hi, (x - hi.astype(F32)).astype(BF16)

    copy.wait()

    lane8 = iota((8, n), 1)
    group = (lane8 % YS) // 4
    quad = lane8 % 4
    lane = iota((YS, n), 1)

    def place(s, b):
        c = code_s[s // 4, (s % 4) * YS + b]
        return jnp.bitwise_and(c, 4095), lax.shift_right_logical(c, 12)

    @pl.loop(0, 8, unroll=2)
    def _(s):
        merged = []
        for g in range(4):
            total = [None] * 4
            for b8 in range(8):
                at, oy_b = place(s, b8 * 4 + g)
                shift = jnp.bitwise_and(4 * b8 - oy_b, n - 1)
                mine = group == b8
                for a in range(4):
                    x = pltpu.roll(pad[pl.ds(at + a * ZR, 8), :], shift, 1)
                    total[a] = jnp.where(mine, x, 0.0 if total[a] is None else total[a])
            merged.append(total)
        cells = []
        for e in range(4):
            for a in range(4):
                x = merged[0][a]
                out = pltpu.roll(x, -e % n, 1) if e else x
                for g in range(1, 4):
                    x = merged[g][a]
                    x = pltpu.roll(x, (g - e) % n, 1) if g != e else x
                    out = jnp.where(quad == g, x, out)
                cells.append(out)
        near[pl.ds(pl.multiple_of(s * n, n), n), :] = jnp.concatenate(cells, axis=0).T

    near_hi, near_lo = split(near[...])
    gas_all = jnp.dot(
        jnp.concatenate([near_hi, near_lo], axis=1), jnp.concatenate([w_hi, w_hi], axis=0), preferred_element_type=F32
    ) + jnp.dot(near_hi, w_lo, preferred_element_type=F32)
    for s in range(8):
        rank, q0 = s // 4, (s % 4) * YS
        row = q0 * ROWS + rank * 5

        def take(k):
            return recv_ref[pl.ds(row + k, YS, stride=ROWS), :]

        head = recv_ref[pl.ds(q0 * ROWS + 10, YS, stride=ROWS), :]
        alive = lane.astype(F32) < head[:, 2 + rank : 3 + rank]
        mass = jnp.where(alive, take(3), 0.0)
        relax = jnp.where(alive, take(4), 1.0)
        drag = TIME_STEP / relax
        under = 1.0 / (1.0 + drag)
        slots = pl.ds(2 * q0 + rank, YS, stride=2)
        for k in range(3):
            gas = gas_all[s * n + k * YS : s * n + (k + 1) * YS]
            settle = TIME_STEP * SETTLING if k == 2 else 0.0
            vel = (take(k) + drag * gas - settle) * under
            force[s * n + k * YS : s * n + (k + 1) * YS, :] = -(mass * drag * (gas - vel))
            pay_ref[k, slots, :] = jnp.where(alive, vel, 0.0)
        pay_ref[3, slots, :] = mass
        pay_ref[4, slots, :] = jnp.where(alive, relax, 0.0)
        force[s * n + 3 * YS : (s + 1) * n, :] = mass
    leave = pltpu.make_async_copy(pay_ref, pay_hbm, pay_sem)
    leave.start()
    across = (((1,), (1,)), ((), ()))
    for s in range(8):
        f_hi, f_lo = split(force[s * n : (s + 1) * n, :])
        near[s * n : (s + 1) * n, :] = lax.dot_general(
            jnp.concatenate([w_hi, w_lo], axis=1),
            jnp.concatenate([f_hi, f_hi], axis=1),
            across,
            preferred_element_type=F32,
        ) + lax.dot_general(w_hi, f_lo, across, preferred_element_type=F32)

    @pl.loop(0, 8)
    def _(s):
        spread = near[pl.ds(pl.multiple_of(s * n, n), n), :]
        for g in range(4):
            parts = []
            for a in range(4):
                out = None
                for e in range(4):
                    x = spread[(e * 4 + a) * 8 : (e * 4 + a) * 8 + 8]
                    x = pltpu.roll(x, (e - g) % n, 1) if e != g else x
                    out = x if out is None else jnp.where(quad == e, x, out)
                parts.append(out)
            for b8 in range(0, 8, 2):
                work = []
                for half, sums in enumerate((acc, more)):
                    at, oy_b = place(s, (b8 + half) * 4 + g)
                    shift = jnp.bitwise_and(oy_b - 4 * (b8 + half), n - 1)
                    mine = group == b8 + half
                    for a in range(4):
                        add = pltpu.roll(jnp.where(mine, parts[a], 0.0), shift, 1)
                        work.append((sums, pl.ds(at + a * ZR, 8), add))
                olds = [sums[rows, :] for sums, rows, _ in work]
                for (sums, rows, add), old in zip(work, olds):
                    sums[rows, :] = old + add

    low, high = 2 * ZR, (planes - 2) * ZR
    sum_ref[...] = acc[low:high, :] + more[low:high, :]
    xlo_ref[...] = acc[0:low, :] + more[0:low, :]
    xhi_ref[...] = acc[high:, :] + more[high:, :]
    leave.wait()


def back_kernel(sum_ref, base_ref, xl_ref, xh_ref, zl_ref, zh_ref, out_ref, ylo_ref, yhi_ref, buf):
    cells_x = sum_ref.shape[0]
    cells_z = out_ref.shape[3]
    cells_y = out_ref.shape[2]
    for x in range(cells_x):
        value = sum_ref[x, ZO : ZO + cells_z, :]
        if x < 2:
            value = value + xl_ref[x, ZO : ZO + cells_z, :]
        if x >= cells_x - 2:
            value = value + xh_ref[x - cells_x + 2, ZO : ZO + cells_z, :]
        buf[x] = value
    buf[:, 0:2, :] += zl_ref[...]
    buf[:, cells_z - 2 : cells_z, :] += zh_ref[...]
    lane = iota((cells_z, LANES), 1)
    inside = (lane % YS >= 2) & (lane % YS < 2 + cells_y)
    for x in range(cells_x):
        flat = (buf[x] + jnp.where(inside, base_ref[x], 0.0)).T
        for k in range(4):
            out_ref[k, x] = flat[k * YS + 2 : k * YS + 2 + cells_y]
            ylo_ref[k, x] = flat[k * YS : k * YS + 2]
            yhi_ref[k, x] = flat[k * YS + 2 + cells_y : k * YS + 4 + cells_y]


def shift_pair(to_low, to_high, axis):
    count = lax.axis_size(axis)
    here = lax.axis_index(axis)
    if axis == "gx":
        up = [(i, (i + 1) % count) for i in range(count)]
        down = [(j, i) for i, j in up]
        low, high = lax.ppermute(to_high, axis, up), lax.ppermute(to_low, axis, down)
    else:
        even = here % 2 == 0
        first = [(i, i + 1 - 2 * (i % 2)) for i in range(count)]
        second = [(i, (i - 1 + 2 * (i % 2)) % count) for i in range(count)]
        one = lax.ppermute(jnp.where(even, to_high, to_low), axis, first)
        two = lax.ppermute(jnp.where(even, to_low, to_high), axis, second)
        low, high = jnp.where(even, two, one), jnp.where(even, one, two)
    return jnp.where(here > 0, low, 0.0), jnp.where(here < count - 1, high, 0.0)


def call(kernel, outs, scratch=(), vmem=40 * 2**20, **kw):
    return pl.pallas_call(
        kernel,
        out_shape=outs,
        scratch_shapes=list(scratch),
        compiler_params=pltpu.CompilerParams(vmem_limit_bytes=vmem),
        **kw,
    )


def arr(*shape, dtype=F32):
    return jax.ShapeDtypeStruct(shape, dtype)


def parcels(recv, mid, z_low, z_high, weight):
    nx = mid.shape[0] - 4
    blocks = recv.shape[0] // ROWS
    rows = (nx + 4) * ZR
    return call(
        parcel_kernel,
        [arr(5, 2 * blocks, LANES), arr(nx * ZR, LANES), arr(2 * ZR, LANES), arr(2 * ZR, LANES)],
        [
            pltpu.VMEM((8, LANES), jnp.int32),
            pltpu.SMEM((8, LANES), jnp.int32),
            pltpu.VMEM((rows, LANES), F32),
            pltpu.VMEM((rows, LANES), F32),
            pltpu.VMEM((rows, LANES), F32),
            pltpu.VMEM((8 * LANES, LANES), F32),
            pltpu.VMEM((8 * LANES, LANES), F32),
            pltpu.VMEM((5, 2 * blocks, LANES), F32),
            pltpu.SemaphoreType.DMA,
            pltpu.SemaphoreType.DMA,
        ],
        out_specs=[pl.BlockSpec(memory_space=pl.ANY)] + [pl.BlockSpec(memory_space=pltpu.VMEM)] * 3,
    )(recv, mid, z_low, z_high, weight)


def per_device(parcel_vel, parcel_props, fill_count, owner_peer, cell_offset, shell_weight, gas_state):
    _, nx, ny, nz = gas_state.shape
    blocks = parcel_vel.shape[0]
    x_low, x_high = shift_pair(gas_state[:, :2], gas_state[:, nx - 2 :], "gx")
    send = call(
        pack_kernel,
        arr(blocks * ROWS, LANES),
        [pltpu.VMEM((1, blocks), jnp.int32)] * 3
        + [
            pltpu.VMEM((3, blocks, LANES), F32),
            pltpu.VMEM((blocks, 2, LANES), F32),
            pltpu.SemaphoreType.DMA((5,)),
        ],
        in_specs=[pl.BlockSpec(memory_space=pltpu.HBM)] * 5,
        vmem=NEARLY_ALL,
    )(
        owner_peer.reshape(1, blocks),
        cell_offset.reshape(1, blocks),
        fill_count.reshape(1, blocks),
        parcel_vel.transpose(1, 0, 2),
        parcel_props,
    )
    send, x_low, x_high = lax.optimization_barrier((send, x_low, x_high))
    recv = lax.all_to_all(
        send.reshape(blocks, ROWS * LANES), ("gx", "gy"), split_axis=0, concat_axis=0, tiled=True
    ).reshape(blocks * ROWS, LANES)
    planes = nx + 4
    rows_buf = [pltpu.VMEM((planes, LANES, nz), F32)]
    z_lo, z_hi = call(edge_kernel, [arr(planes, 2, LANES)] * 2, rows_buf)(gas_state, x_low, x_high)
    z_low, z_high = shift_pair(z_lo, z_hi, "gz")

    def y_face(lo):
        parts = [part[:, :, lo : lo + 2] for part in (x_low, gas_state, x_high)]
        face = jnp.concatenate(parts, axis=1).reshape(8 * planes, nz)
        return jnp.concatenate([face, z_low.reshape(2 * planes, LANES), z_high.reshape(2 * planes, LANES)], axis=0)

    y_low, y_high = shift_pair(y_face(0), y_face(ny - 2), "gy")
    halo = call(turn_kernel, [arr(planes, nz, LANES), arr(planes, 2, LANES), arr(planes, 2, LANES)], rows_buf)(
        gas_state, x_low, x_high, z_low, z_high, y_low, y_high
    )

    weight = shell_weight.reshape(LANES, 4, 4, 8).transpose(2, 1, 3, 0).reshape(LANES, LANES)
    pay, total, x_lo, x_hi = parcels(recv, *halo, weight)
    parcels_next = pay.transpose(1, 0, 2)
    base = call(diffuse_kernel, arr(nx, nz, LANES), [pltpu.VMEM((2, ZR, LANES), F32)])(*halo)

    from_low, from_high = shift_pair(x_lo.reshape(2, ZR, LANES), x_hi.reshape(2, ZR, LANES), "gx")
    total = total.reshape(nx, ZR, LANES)

    def rim(lo, hi):
        part = total[:, lo:hi]
        return jnp.concatenate(
            [part[:2] + from_low[:, lo:hi], part[2 : nx - 2], part[nx - 2 :] + from_high[:, lo:hi]], axis=0
        )

    z_below, z_above = shift_pair(rim(ZO - 2, ZO), rim(ZO + nz, ZO + nz + 2), "gz")
    rows_out, y_lo, y_hi = call(
        back_kernel,
        [arr(4, nx, ny, nz), arr(4, nx, 2, nz), arr(4, nx, 2, nz)],
        [pltpu.VMEM((nx, nz, LANES), F32)],
    )(total, base, from_low, from_high, z_below, z_above)
    y_below, y_above = shift_pair(y_lo, y_hi, "gy")
    gas_next = jnp.concatenate(
        [rows_out[:, :, :2] + y_below, rows_out[:, :, 2 : ny - 2], rows_out[:, :, ny - 2 :] + y_above], axis=2
    )
    return parcels_next, gas_next


def solution(mesh):
    return jax.shard_map(
        per_device,
        mesh=mesh,
        in_specs=(
            P(("gx", "gy", "gz"), None, None),
            P(("gx", "gy", "gz"), None, None),
            P(("gx", "gy", "gz")),
            P(("gx", "gy", "gz"), None),
            P(("gx", "gy", "gz")),
            P(),
            P(None, "gx", "gy", "gz"),
        ),
        out_specs=(P(("gx", "gy", "gz"), None, None), P(None, "gx", "gy", "gz")),
        check_vma=False,
    )
```

```python
import functools
import jax
import jax.numpy as jnp
from jax import lax
from jax.experimental import pallas as pl
from jax.experimental.pallas import tpu as pltpu
from jax.sharding import PartitionSpec as P

TIME_STEP = 0.05
SETTLING = 1.0
F32 = jnp.float32
BF16 = jnp.bfloat16
HI = lax.Precision.HIGHEST

LANES = 128
NEARLY_ALL = 66200000
ROWS = 11
ZR = 144
ZO = 8
YS = 32


def iota(shape, dim):
    return lax.broadcasted_iota(jnp.int32, shape, dim)


def pack_kernel(tgt_hbm, off_hbm, cnt_hbm, vel_hbm, prop_hbm, out_ref, tgt_ref, off_ref, cnt_ref, vel_ref, prop_ref, sems):
    n = LANES
    pairs = ((tgt_hbm, tgt_ref), (off_hbm, off_ref), (cnt_hbm, cnt_ref), (vel_hbm, vel_ref), (prop_hbm, prop_ref))
    copies = [pltpu.make_async_copy(src, dst, sems.at[i]) for i, (src, dst) in enumerate(pairs)]
    for copy in copies:
        copy.start()
    for copy in copies[:3]:
        copy.wait()
    hot = (iota((n, n), 0) == tgt_ref[...]).astype(F32)
    earlier = (iota((n, n), 0) < iota((n, n), 1)).astype(BF16)
    rank = jnp.dot(hot.astype(BF16), earlier, preferred_element_type=F32)
    first = jnp.where(rank < 0.5, hot, 0.0)
    second = jnp.where(rank > 0.5, hot, 0.0)
    off = off_ref[...].astype(F32)
    cnt = cnt_ref[...].astype(F32)
    lane = iota((n, n), 1)
    head = jnp.zeros((n, n), F32)
    for place, (pick, val) in enumerate(((first, off), (second, off), (first, cnt), (second, cnt))):
        column = jnp.sum(pick * val, axis=1, keepdims=True)
        head = jnp.where(lane == place, column, head)
    out_ref[pl.ds(10, n, stride=ROWS), :] = head
    picks = jnp.concatenate([first, second], axis=0).astype(BF16)
    for copy in copies[3:]:
        copy.wait()
    for k in range(5):
        x = vel_ref[k] if k < 3 else prop_ref[:, k - 3, :]
        total = jnp.zeros((2 * n, n), F32)
        for _ in range(3):
            part = x.astype(BF16)
            x = x - part.astype(F32)
            total = total + jnp.dot(picks, part, preferred_element_type=F32)
        out_ref[pl.ds(k, n, stride=ROWS), :] = total[:n]
        out_ref[pl.ds(5 + k, n, stride=ROWS), :] = total[n:]


def fill_rows(buf, gas_ref, xl_ref, xh_ref):
    cells_x, cells_y = gas_ref.shape[1], gas_ref.shape[2]
    for x in range(cells_x + 4):
        ref, at = (xl_ref, x) if x < 2 else (gas_ref, x - 2) if x < cells_x + 2 else (xh_ref, x - cells_x - 2)
        for k in range(4):
            buf[x, k * YS + 2 : k * YS + 2 + cells_y, :] = ref[k, at]


def edge_kernel(gas_ref, xl_ref, xh_ref, lo_ref, hi_ref, buf):
    cells_z = gas_ref.shape[3]
    buf[...] = jnp.zeros_like(buf)
    fill_rows(buf, gas_ref, xl_ref, xh_ref)
    for x in range(lo_ref.shape[0]):
        flat = buf[x].T
        lo_ref[x] = flat[0:2]
        hi_ref[x] = flat[cells_z - 2 : cells_z]


def turn_kernel(gas_ref, xl_ref, xh_ref, zl_ref, zh_ref, yl_ref, yh_ref, out_ref, buf):
    planes, cells_y, cells_z = out_ref.shape[0], gas_ref.shape[2], gas_ref.shape[3]
    buf[...] = jnp.zeros_like(buf)
    fill_rows(buf, gas_ref, xl_ref, xh_ref)
    y = iota((2, LANES), 1) % YS
    for x in range(planes):
        for k in range(4):
            row = (k * planes + x) * 2
            buf[x, k * YS : k * YS + 2, :] = yl_ref[row : row + 2]
            buf[x, k * YS + 2 + cells_y : k * YS + 4 + cells_y, :] = yh_ref[row : row + 2]
        for part, z_ref in enumerate((zl_ref, zh_ref)):
            row = (4 + part) * planes * 2 + x * 2
            below = pltpu.roll(yl_ref[row : row + 2], LANES - cells_y, 1)
            above = pltpu.roll(yh_ref[row : row + 2], cells_y, 1)
            at = ZO - 2 + part * (cells_z + 2)
            out_ref[x, at : at + 2, :] = jnp.where(
                y < 2, below, jnp.where(y < 2 + cells_y, z_ref[x], jnp.where(y < 4 + cells_y, above, 0.0))
            )
    for x in range(planes):
        out_ref[x, ZO : ZO + cells_z, :] = buf[x].T


def diffuse_kernel(pad_ref, out_ref):
    cells_x, cells_z = out_ref.shape[0], out_ref.shape[1]
    last = ZO + cells_z
    lane = iota((cells_z, LANES), 1)
    rate = jnp.where(lane < 3 * YS, TIME_STEP, 0.5 * TIME_STEP).astype(F32)
    for x in range(2, cells_x + 2):
        here = pad_ref[x, ZO:last, :]
        beside = pad_ref[x - 1, ZO:last, :] + pad_ref[x + 1, ZO:last, :]
        beside = beside + pltpu.roll(here, LANES - 1, 1) + pltpu.roll(here, 1, 1)
        beside = beside + pad_ref[x, ZO + 1 : last + 1, :] + pad_ref[x, ZO - 1 : last - 1, :]
        out_ref[x - 2] = here + rate * (beside - 6.0 * here)


def parcel_kernel(
    recv_ref, pad, w_ref,
    pay_hbm, sum_ref, xlo_ref, xhi_ref,
    code_v, code_s, acc, more, near, force, pay_ref, sem, pay_sem,
):
    planes = pad.shape[0] // ZR
    n = LANES
    off = recv_ref[pl.ds(10, n, stride=ROWS), :]
    rest = jnp.floor((off + 0.5) * (1.0 / 125.0))
    oz = off - rest * 125.0
    ox = jnp.floor((rest + 0.5) * (1.0 / 17.0))
    oy = rest - ox * 17.0
    code = oy * 4096.0 + ox * float(ZR) + oz + float(ZO - 2)
    code_v[...] = code.T[0:8].astype(jnp.int32)
    copy = pltpu.make_async_copy(code_v, code_s, sem)
    copy.start()
    acc[...] = jnp.zeros_like(acc)
    more[...] = jnp.zeros_like(more)
    w_hi = w_ref[...].astype(BF16)
    w_lo = (w_ref[...] - w_hi.astype(F32)).astype(BF16)

    def split(x):
        hi = x.astype(BF16)
        return hi, (x - hi.astype(F32)).astype(BF16)

    copy.wait()

    lane8 = iota((8, n), 1)
    group = (lane8 % YS) // 4
    quad = lane8 % 4
    lane = iota((YS, n), 1)

    def place(s, b):
        c = code_s[s // 4, (s % 4) * YS + b]
        return jnp.bitwise_and(c, 4095), lax.shift_right_logical(c, 12)

    @pl.loop(0, 8, unroll=2)
    def _(s):
        merged = []
        for g in range(4):
            total = [None] * 4
            for b8 in range(8):
                at, oy_b = place(s, b8 * 4 + g)
                shift = jnp.bitwise_and(4 * b8 - oy_b, n - 1)
                mine = group == b8
                for a in range(4):
                    x = pltpu.roll(pad[pl.ds(at + a * ZR, 8), :], shift, 1)
                    total[a] = jnp.where(mine, x, 0.0 if total[a] is None else total[a])
            merged.append(total)
        cells = []
        for e in range(4):
            for a in range(4):
                x = merged[0][a]
                out = pltpu.roll(x, -e % n, 1) if e else x
                for g in range(1, 4):
                    x = merged[g][a]
                    x = pltpu.roll(x, (g - e) % n, 1) if g != e else x
                    out = jnp.where(quad == g, x, out)
                cells.append(out)
        near[pl.ds(pl.multiple_of(s * n, n), n), :] = jnp.concatenate(cells, axis=0).T

    near_hi, near_lo = split(near[...])
    gas_all = jnp.dot(
        jnp.concatenate([near_hi, near_lo], axis=1), jnp.concatenate([w_hi, w_hi], axis=0), preferred_element_type=F32
    ) + jnp.dot(near_hi, w_lo, preferred_element_type=F32)
    for s in range(8):
        rank, q0 = s // 4, (s % 4) * YS
        row = q0 * ROWS + rank * 5

        def take(k):
            return recv_ref[pl.ds(row + k, YS, stride=ROWS), :]

        head = recv_ref[pl.ds(q0 * ROWS + 10, YS, stride=ROWS), :]
        alive = lane.astype(F32) < head[:, 2 + rank : 3 + rank]
        mass = jnp.where(alive, take(3), 0.0)
        relax = jnp.where(alive, take(4), 1.0)
        drag = TIME_STEP / relax
        under = 1.0 / (1.0 + drag)
        slots = pl.ds(2 * q0 + rank, YS, stride=2)
        for k in range(3):
            gas = gas_all[s * n + k * YS : s * n + (k + 1) * YS]
            settle = TIME_STEP * SETTLING if k == 2 else 0.0
            vel = (take(k) + drag * gas - settle) * under
            force[s * n + k * YS : s * n + (k + 1) * YS, :] = -(mass * drag * (gas - vel))
            pay_ref[k, slots, :] = jnp.where(alive, vel, 0.0)
        pay_ref[3, slots, :] = mass
        pay_ref[4, slots, :] = jnp.where(alive, relax, 0.0)
        force[s * n + 3 * YS : (s + 1) * n, :] = mass
    leave = pltpu.make_async_copy(pay_ref, pay_hbm, pay_sem)
    leave.start()
    across = (((1,), (1,)), ((), ()))
    for s in range(8):
        f_hi, f_lo = split(force[s * n : (s + 1) * n, :])
        near[s * n : (s + 1) * n, :] = lax.dot_general(
            jnp.concatenate([w_hi, w_lo], axis=1),
            jnp.concatenate([f_hi, f_hi], axis=1),
            across,
            preferred_element_type=F32,
        ) + lax.dot_general(w_hi, f_lo, across, preferred_element_type=F32)

    @pl.loop(0, 8)
    def _(s):
        spread = near[pl.ds(pl.multiple_of(s * n, n), n), :]
        for g in range(4):
            parts = []
            for a in range(4):
                out = None
                for e in range(4):
                    x = spread[(e * 4 + a) * 8 : (e * 4 + a) * 8 + 8]
                    x = pltpu.roll(x, (e - g) % n, 1) if e != g else x
                    out = x if out is None else jnp.where(quad == e, x, out)
                parts.append(out)
            for b8 in range(0, 8, 2):
                work = []
                for half, sums in enumerate((acc, more)):
                    at, oy_b = place(s, (b8 + half) * 4 + g)
                    shift = jnp.bitwise_and(oy_b - 4 * (b8 + half), n - 1)
                    mine = group == b8 + half
                    for a in range(4):
                        add = pltpu.roll(jnp.where(mine, parts[a], 0.0), shift, 1)
                        work.append((sums, pl.ds(at + a * ZR, 8), add))
                olds = [sums[rows, :] for sums, rows, _ in work]
                for (sums, rows, add), old in zip(work, olds):
                    sums[rows, :] = old + add

    low, high = 2 * ZR, (planes - 2) * ZR
    sum_ref[...] = acc[low:high, :] + more[low:high, :]
    xlo_ref[...] = acc[0:low, :] + more[0:low, :]
    xhi_ref[...] = acc[high:, :] + more[high:, :]
    leave.wait()


def back_kernel(sum_ref, base_ref, xl_ref, xh_ref, zl_ref, zh_ref, out_ref, ylo_ref, yhi_ref, buf):
    cells_x = sum_ref.shape[0]
    cells_z = out_ref.shape[3]
    cells_y = out_ref.shape[2]
    for x in range(cells_x):
        value = sum_ref[x, ZO : ZO + cells_z, :]
        if x < 2:
            value = value + xl_ref[x, ZO : ZO + cells_z, :]
        if x >= cells_x - 2:
            value = value + xh_ref[x - cells_x + 2, ZO : ZO + cells_z, :]
        buf[x] = value
    buf[:, 0:2, :] += zl_ref[...]
    buf[:, cells_z - 2 : cells_z, :] += zh_ref[...]
    lane = iota((cells_z, LANES), 1)
    inside = (lane % YS >= 2) & (lane % YS < 2 + cells_y)
    for x in range(cells_x):
        flat = (buf[x] + jnp.where(inside, base_ref[x], 0.0)).T
        for k in range(4):
            out_ref[k, x] = flat[k * YS + 2 : k * YS + 2 + cells_y]
            ylo_ref[k, x] = flat[k * YS : k * YS + 2]
            yhi_ref[k, x] = flat[k * YS + 2 + cells_y : k * YS + 4 + cells_y]


def shift_pair(to_low, to_high, axis, ring=False):
    count = lax.axis_size(axis)
    if not ring:
        up = [(i, i + 1) for i in range(count - 1)]
        down = [(j, i) for i, j in up]
        return lax.ppermute(to_high, axis, up), lax.ppermute(to_low, axis, down)
    up = [(i, (i + 1) % count) for i in range(count)]
    down = [(j, i) for i, j in up]
    here = lax.axis_index(axis)
    low, high = lax.ppermute(to_high, axis, up), lax.ppermute(to_low, axis, down)
    return jnp.where(here > 0, low, 0.0), jnp.where(here < count - 1, high, 0.0)


def call(kernel, outs, scratch=(), vmem=40 * 2**20, **kw):
    return pl.pallas_call(
        kernel,
        out_shape=outs,
        scratch_shapes=list(scratch),
        compiler_params=pltpu.CompilerParams(vmem_limit_bytes=vmem),
        **kw,
    )


def arr(*shape, dtype=F32):
    return jax.ShapeDtypeStruct(shape, dtype)


def parcels(recv, padded, weight):
    rows = padded.shape[0]
    nx = rows // ZR - 4
    blocks = recv.shape[0] // ROWS
    return call(
        parcel_kernel,
        [arr(5, 2 * blocks, LANES), arr(nx * ZR, LANES), arr(2 * ZR, LANES), arr(2 * ZR, LANES)],
        [
            pltpu.VMEM((8, LANES), jnp.int32),
            pltpu.SMEM((8, LANES), jnp.int32),
            pltpu.VMEM((rows, LANES), F32),
            pltpu.VMEM((rows, LANES), F32),
            pltpu.VMEM((8 * LANES, LANES), F32),
            pltpu.VMEM((8 * LANES, LANES), F32),
            pltpu.VMEM((5, 2 * blocks, LANES), F32),
            pltpu.SemaphoreType.DMA,
            pltpu.SemaphoreType.DMA,
        ],
        out_specs=[pl.BlockSpec(memory_space=pl.ANY)] + [pl.BlockSpec(memory_space=pltpu.VMEM)] * 3,
    )(recv, padded, weight)


def per_device(parcel_vel, parcel_props, fill_count, owner_peer, cell_offset, shell_weight, gas_state):
    _, nx, ny, nz = gas_state.shape
    blocks = parcel_vel.shape[0]
    x_low, x_high = shift_pair(gas_state[:, :2], gas_state[:, nx - 2 :], "gx", ring=True)
    send = call(
        pack_kernel,
        arr(blocks * ROWS, LANES),
        [pltpu.VMEM((1, blocks), jnp.int32)] * 3
        + [
            pltpu.VMEM((3, blocks, LANES), F32),
            pltpu.VMEM((blocks, 2, LANES), F32),
            pltpu.SemaphoreType.DMA((5,)),
        ],
        in_specs=[pl.BlockSpec(memory_space=pltpu.HBM)] * 5,
        vmem=NEARLY_ALL,
    )(
        owner_peer.reshape(1, blocks),
        cell_offset.reshape(1, blocks),
        fill_count.reshape(1, blocks),
        parcel_vel.transpose(1, 0, 2),
        parcel_props,
    )
    send, x_low, x_high = lax.optimization_barrier((send, x_low, x_high))
    recv = lax.all_to_all(
        send.reshape(blocks, ROWS * LANES), ("gx", "gy"), split_axis=0, concat_axis=0, tiled=True
    ).reshape(blocks * ROWS, LANES)
    planes = nx + 4
    rows_buf = [pltpu.VMEM((planes, LANES, nz), F32)]
    z_lo, z_hi = call(edge_kernel, [arr(planes, 2, LANES)] * 2, rows_buf)(gas_state, x_low, x_high)
    z_low, z_high = shift_pair(z_lo, z_hi, "gz")

    def y_face(lo):
        parts = [part[:, :, lo : lo + 2] for part in (x_low, gas_state, x_high)]
        face = jnp.concatenate(parts, axis=1).reshape(8 * planes, nz)
        return jnp.concatenate([face, z_low.reshape(2 * planes, LANES), z_high.reshape(2 * planes, LANES)], axis=0)

    y_low, y_high = shift_pair(y_face(0), y_face(ny - 2), "gy")
    padded = call(turn_kernel, arr(planes, ZR, LANES), rows_buf)(
        gas_state, x_low, x_high, z_low, z_high, y_low, y_high
    )

    weight = shell_weight.reshape(LANES, 4, 4, 8).transpose(2, 1, 3, 0).reshape(LANES, LANES)
    pay, total, x_lo, x_hi = parcels(recv, padded.reshape(planes * ZR, LANES), weight)
    parcels_next = pay.transpose(1, 0, 2)
    base = call(diffuse_kernel, arr(nx, nz, LANES))(padded)

    from_low, from_high = shift_pair(x_lo.reshape(2, ZR, LANES), x_hi.reshape(2, ZR, LANES), "gx", ring=True)
    total = total.reshape(nx, ZR, LANES)

    def rim(lo, hi):
        part = total[:, lo:hi]
        return jnp.concatenate(
            [part[:2] + from_low[:, lo:hi], part[2 : nx - 2], part[nx - 2 :] + from_high[:, lo:hi]], axis=0
        )

    z_below, z_above = shift_pair(rim(ZO - 2, ZO), rim(ZO + nz, ZO + nz + 2), "gz")
    rows_out, y_lo, y_hi = call(
        back_kernel,
        [arr(4, nx, ny, nz), arr(4, nx, 2, nz), arr(4, nx, 2, nz)],
        [pltpu.VMEM((nx, nz, LANES), F32)],
    )(total, base, from_low, from_high, z_below, z_above)
    y_below, y_above = shift_pair(y_lo, y_hi, "gy")
    gas_next = jnp.concatenate(
        [rows_out[:, :, :2] + y_below, rows_out[:, :, 2 : ny - 2], rows_out[:, :, ny - 2 :] + y_above], axis=2
    )
    return parcels_next, gas_next


def solution(mesh):
    return jax.shard_map(
        per_device,
        mesh=mesh,
        in_specs=(
            P(("gx", "gy", "gz"), None, None),
            P(("gx", "gy", "gz"), None, None),
            P(("gx", "gy", "gz")),
            P(("gx", "gy", "gz"), None),
            P(("gx", "gy", "gz")),
            P(),
            P(None, "gx", "gy", "gz"),
        ),
        out_specs=(P(("gx", "gy", "gz"), None, None), P(None, "gx", "gy", "gz")),
        check_vma=False,
    )
```

```python
import functools
import jax
import jax.numpy as jnp
from jax import lax
from jax.experimental import pallas as pl
from jax.experimental.pallas import tpu as pltpu
from jax.sharding import PartitionSpec as P

TIME_STEP = 0.05
SETTLING = 1.0
F32 = jnp.float32
BF16 = jnp.bfloat16
HI = lax.Precision.HIGHEST

LANES = 128
NEARLY_ALL = 66200000
ROWS = 11
ZR = 144
ZO = 8
YS = 32


def iota(shape, dim):
    return lax.broadcasted_iota(jnp.int32, shape, dim)


def pack_kernel(tgt_hbm, off_hbm, cnt_hbm, vel_hbm, prop_hbm, out_ref, tgt_ref, off_ref, cnt_ref, vel_ref, prop_ref, sems):
    n = LANES
    pairs = ((tgt_hbm, tgt_ref), (off_hbm, off_ref), (cnt_hbm, cnt_ref), (vel_hbm, vel_ref), (prop_hbm, prop_ref))
    copies = [pltpu.make_async_copy(src, dst, sems.at[i]) for i, (src, dst) in enumerate(pairs)]
    for copy in copies:
        copy.start()
    for copy in copies[:3]:
        copy.wait()
    hot = (iota((n, n), 0) == tgt_ref[...]).astype(F32)
    earlier = (iota((n, n), 0) < iota((n, n), 1)).astype(BF16)
    rank = jnp.dot(hot.astype(BF16), earlier, preferred_element_type=F32)
    first = jnp.where(rank < 0.5, hot, 0.0)
    second = jnp.where(rank > 0.5, hot, 0.0)
    off = off_ref[...].astype(F32)
    cnt = cnt_ref[...].astype(F32)
    lane = iota((n, n), 1)
    head = jnp.zeros((n, n), F32)
    for place, (pick, val) in enumerate(((first, off), (second, off), (first, cnt), (second, cnt))):
        column = jnp.sum(pick * val, axis=1, keepdims=True)
        head = jnp.where(lane == place, column, head)
    out_ref[pl.ds(10, n, stride=ROWS), :] = head
    picks = jnp.concatenate([first, second], axis=0).astype(BF16)
    for copy in copies[3:]:
        copy.wait()
    for k in range(5):
        x = vel_ref[k] if k < 3 else prop_ref[:, k - 3, :]
        total = jnp.zeros((2 * n, n), F32)
        for _ in range(3):
            part = x.astype(BF16)
            x = x - part.astype(F32)
            total = total + jnp.dot(picks, part, preferred_element_type=F32)
        out_ref[pl.ds(k, n, stride=ROWS), :] = total[:n]
        out_ref[pl.ds(5 + k, n, stride=ROWS), :] = total[n:]


def fill_rows(buf, gas_ref, xl_ref, xh_ref):
    cells_x, cells_y = gas_ref.shape[1], gas_ref.shape[2]
    for x in range(cells_x + 4):
        ref, at = (xl_ref, x) if x < 2 else (gas_ref, x - 2) if x < cells_x + 2 else (xh_ref, x - cells_x - 2)
        for k in range(4):
            buf[x, k * YS + 2 : k * YS + 2 + cells_y, :] = ref[k, at]


def edge_kernel(gas_ref, xl_ref, xh_ref, lo_ref, hi_ref, buf):
    cells_z = gas_ref.shape[3]
    buf[...] = jnp.zeros_like(buf)
    fill_rows(buf, gas_ref, xl_ref, xh_ref)
    for x in range(lo_ref.shape[0]):
        flat = buf[x].T
        lo_ref[x] = flat[0:2]
        hi_ref[x] = flat[cells_z - 2 : cells_z]


SIDE = 8


def yface_kernel(gas_ref, xl_ref, xh_ref, zl_ref, zh_ref, lo_ref, hi_ref):
    cells_x, cells_y = gas_ref.shape[1], gas_ref.shape[2]
    planes = cells_x + 4
    each = planes // (SIDE // 2)
    for ref, at in ((lo_ref, 0), (hi_ref, cells_y - 2)):
        for k in range(4):
            ref[k * planes : k * planes + 2] = xl_ref[k, :, at : at + 2, :]
            ref[k * planes + 2 : k * planes + 2 + cells_x] = gas_ref[k, :, at : at + 2, :]
            ref[k * planes + 2 + cells_x : (k + 1) * planes] = xh_ref[k, :, at : at + 2, :]
        total = None
        for m in range(SIDE):
            z_ref, first = (zl_ref, m) if m < SIDE // 2 else (zh_ref, m - SIDE // 2)
            rows = z_ref[first * each : (first + 1) * each].reshape(2 * each, LANES)
            rows = pltpu.roll(rows, (4 * m - 2 - at) % LANES, 1)
            y = iota(rows.shape, 1) % YS
            total = jnp.where((y >= 4 * m) & (y < 4 * m + 2), rows, 0.0 if total is None else total)
        ref[4 * planes : 4 * planes + each] = total.reshape(each, 2, LANES)


def turn_kernel(gas_ref, xl_ref, xh_ref, zl_ref, zh_ref, yl_ref, yh_ref, out_ref, buf):
    planes, cells_y, cells_z = out_ref.shape[0], gas_ref.shape[2], gas_ref.shape[3]
    each = planes // (SIDE // 2)
    buf[...] = jnp.zeros_like(buf)
    fill_rows(buf, gas_ref, xl_ref, xh_ref)
    for x in range(planes):
        for k in range(4):
            buf[x, k * YS : k * YS + 2, :] = yl_ref[k * planes + x]
            buf[x, k * YS + 2 + cells_y : k * YS + 4 + cells_y, :] = yh_ref[k * planes + x]
    below, above = (ref[4 * planes : 4 * planes + each].reshape(2 * each, LANES) for ref in (yl_ref, yh_ref))
    y = iota((2 * each, LANES), 1) % YS
    for m in range(SIDE):
        z_ref, first = (zl_ref, m) if m < SIDE // 2 else (zh_ref, m - SIDE // 2)
        inner = z_ref[first * each : (first + 1) * each].reshape(2 * each, LANES)
        low = pltpu.roll(below, -4 * m % LANES, 1)
        high = pltpu.roll(above, (2 + cells_y - 4 * m) % LANES, 1)
        rows = jnp.where(y < 2, low, jnp.where(y < 2 + cells_y, inner, jnp.where(y < 4 + cells_y, high, 0.0)))
        at = ZO - 2 if m < SIDE // 2 else ZO + cells_z
        for x in range(each):
            out_ref[first * each + x, at : at + 2, :] = rows[2 * x : 2 * x + 2]
    for x in range(planes):
        out_ref[x, ZO : ZO + cells_z, :] = buf[x].T


def diffuse_kernel(pad_ref, out_ref):
    cells_x, cells_z = out_ref.shape[0], out_ref.shape[1]
    last = ZO + cells_z
    lane = iota((cells_z, LANES), 1)
    rate = jnp.where(lane < 3 * YS, TIME_STEP, 0.5 * TIME_STEP).astype(F32)
    for x in range(2, cells_x + 2):
        here = pad_ref[x, ZO:last, :]
        beside = pad_ref[x - 1, ZO:last, :] + pad_ref[x + 1, ZO:last, :]
        beside = beside + pltpu.roll(here, LANES - 1, 1) + pltpu.roll(here, 1, 1)
        beside = beside + pad_ref[x, ZO + 1 : last + 1, :] + pad_ref[x, ZO - 1 : last - 1, :]
        out_ref[x - 2] = here + rate * (beside - 6.0 * here)


def parcel_kernel(
    recv_ref, pad, w_ref,
    pay_hbm, sum_ref, xlo_ref, xhi_ref,
    code_v, code_s, acc, more, near, force, pay_ref, sem, pay_sem,
):
    planes = pad.shape[0] // ZR
    n = LANES
    off = recv_ref[pl.ds(10, n, stride=ROWS), :]
    rest = jnp.floor((off + 0.5) * (1.0 / 125.0))
    oz = off - rest * 125.0
    ox = jnp.floor((rest + 0.5) * (1.0 / 17.0))
    oy = rest - ox * 17.0
    code = oy * 4096.0 + ox * float(ZR) + oz + float(ZO - 2)
    code_v[...] = code.T[0:8].astype(jnp.int32)
    copy = pltpu.make_async_copy(code_v, code_s, sem)
    copy.start()
    acc[...] = jnp.zeros_like(acc)
    more[...] = jnp.zeros_like(more)
    w_hi = w_ref[...].astype(BF16)
    w_lo = (w_ref[...] - w_hi.astype(F32)).astype(BF16)

    def split(x):
        hi = x.astype(BF16)
        return hi, (x - hi.astype(F32)).astype(BF16)

    copy.wait()

    lane8 = iota((8, n), 1)
    group = (lane8 % YS) // 4
    quad = lane8 % 4
    lane = iota((YS, n), 1)

    def place(s, b):
        c = code_s[s // 4, (s % 4) * YS + b]
        return jnp.bitwise_and(c, 4095), lax.shift_right_logical(c, 12)

    @pl.loop(0, 8, unroll=2)
    def _(s):
        merged = []
        for g in range(4):
            total = [None] * 4
            for b8 in range(8):
                at, oy_b = place(s, b8 * 4 + g)
                shift = jnp.bitwise_and(4 * b8 - oy_b, n - 1)
                mine = group == b8
                for a in range(4):
                    x = pltpu.roll(pad[pl.ds(at + a * ZR, 8), :], shift, 1)
                    total[a] = jnp.where(mine, x, 0.0 if total[a] is None else total[a])
            merged.append(total)
        cells = []
        for e in range(4):
            for a in range(4):
                x = merged[0][a]
                out = pltpu.roll(x, -e % n, 1) if e else x
                for g in range(1, 4):
                    x = merged[g][a]
                    x = pltpu.roll(x, (g - e) % n, 1) if g != e else x
                    out = jnp.where(quad == g, x, out)
                cells.append(out)
        near[pl.ds(pl.multiple_of(s * n, n), n), :] = jnp.concatenate(cells, axis=0).T

    near_hi, near_lo = split(near[...])
    gas_all = jnp.dot(
        jnp.concatenate([near_hi, near_lo], axis=1), jnp.concatenate([w_hi, w_hi], axis=0), preferred_element_type=F32
    ) + jnp.dot(near_hi, w_lo, preferred_element_type=F32)
    for s in range(8):
        rank, q0 = s // 4, (s % 4) * YS
        row = q0 * ROWS + rank * 5

        def take(k):
            return recv_ref[pl.ds(row + k, YS, stride=ROWS), :]

        head = recv_ref[pl.ds(q0 * ROWS + 10, YS, stride=ROWS), :]
        alive = lane.astype(F32) < head[:, 2 + rank : 3 + rank]
        mass = jnp.where(alive, take(3), 0.0)
        relax = jnp.where(alive, take(4), 1.0)
        drag = TIME_STEP / relax
        under = 1.0 / (1.0 + drag)
        slots = pl.ds(2 * q0 + rank, YS, stride=2)
        for k in range(3):
            gas = gas_all[s * n + k * YS : s * n + (k + 1) * YS]
            settle = TIME_STEP * SETTLING if k == 2 else 0.0
            vel = (take(k) + drag * gas - settle) * under
            force[s * n + k * YS : s * n + (k + 1) * YS, :] = -(mass * drag * (gas - vel))
            pay_ref[k, slots, :] = jnp.where(alive, vel, 0.0)
        pay_ref[3, slots, :] = mass
        pay_ref[4, slots, :] = jnp.where(alive, relax, 0.0)
        force[s * n + 3 * YS : (s + 1) * n, :] = mass
    leave = pltpu.make_async_copy(pay_ref, pay_hbm, pay_sem)
    leave.start()
    across = (((1,), (1,)), ((), ()))
    for s in range(8):
        f_hi, f_lo = split(force[s * n : (s + 1) * n, :])
        near[s * n : (s + 1) * n, :] = lax.dot_general(
            jnp.concatenate([w_hi, w_lo], axis=1),
            jnp.concatenate([f_hi, f_hi], axis=1),
            across,
            preferred_element_type=F32,
        ) + lax.dot_general(w_hi, f_lo, across, preferred_element_type=F32)

    @pl.loop(0, 8)
    def _(s):
        spread = near[pl.ds(pl.multiple_of(s * n, n), n), :]
        for g in range(4):
            parts = []
            for a in range(4):
                out = None
                for e in range(4):
                    x = spread[(e * 4 + a) * 8 : (e * 4 + a) * 8 + 8]
                    x = pltpu.roll(x, (e - g) % n, 1) if e != g else x
                    out = x if out is None else jnp.where(quad == e, x, out)
                parts.append(out)
            for b8 in range(0, 8, 2):
                work = []
                for half, sums in enumerate((acc, more)):
                    at, oy_b = place(s, (b8 + half) * 4 + g)
                    shift = jnp.bitwise_and(oy_b - 4 * (b8 + half), n - 1)
                    mine = group == b8 + half
                    for a in range(4):
                        add = pltpu.roll(jnp.where(mine, parts[a], 0.0), shift, 1)
                        work.append((sums, pl.ds(at + a * ZR, 8), add))
                olds = [sums[rows, :] for sums, rows, _ in work]
                for (sums, rows, add), old in zip(work, olds):
                    sums[rows, :] = old + add

    low, high = 2 * ZR, (planes - 2) * ZR
    sum_ref[...] = acc[low:high, :] + more[low:high, :]
    xlo_ref[...] = acc[0:low, :] + more[0:low, :]
    xhi_ref[...] = acc[high:, :] + more[high:, :]
    leave.wait()


def back_kernel(sum_ref, base_ref, xl_ref, xh_ref, zl_ref, zh_ref, out_ref, ylo_ref, yhi_ref, buf):
    cells_x = sum_ref.shape[0]
    cells_z = out_ref.shape[3]
    cells_y = out_ref.shape[2]
    for x in range(cells_x):
        value = sum_ref[x, ZO : ZO + cells_z, :]
        if x < 2:
            value = value + xl_ref[x, ZO : ZO + cells_z, :]
        if x >= cells_x - 2:
            value = value + xh_ref[x - cells_x + 2, ZO : ZO + cells_z, :]
        buf[x] = value
    buf[:, 0:2, :] += zl_ref[...]
    buf[:, cells_z - 2 : cells_z, :] += zh_ref[...]
    lane = iota((cells_z, LANES), 1)
    inside = (lane % YS >= 2) & (lane % YS < 2 + cells_y)
    for x in range(cells_x):
        flat = (buf[x] + jnp.where(inside, base_ref[x], 0.0)).T
        for k in range(4):
            out_ref[k, x] = flat[k * YS + 2 : k * YS + 2 + cells_y]
            ylo_ref[k, x] = flat[k * YS : k * YS + 2]
            yhi_ref[k, x] = flat[k * YS + 2 + cells_y : k * YS + 4 + cells_y]


def last_kernel(rows_ref, below_ref, above_ref, out_hbm, buf, sems):
    cells_y = rows_ref.shape[2]
    copies = []
    for k in range(4):
        buf[k] = rows_ref[k]
        buf[k, :, 0:2, :] += below_ref[k]
        buf[k, :, cells_y - 2 : cells_y, :] += above_ref[k]
        copies.append(pltpu.make_async_copy(buf.at[k], out_hbm.at[k], sems.at[k]))
        copies[-1].start()
    for copy in copies:
        copy.wait()


def shift_pair(to_low, to_high, axis, ring=False):
    count = lax.axis_size(axis)
    if not ring:
        up = [(i, i + 1) for i in range(count - 1)]
        down = [(j, i) for i, j in up]
        return lax.ppermute(to_high, axis, up), lax.ppermute(to_low, axis, down)
    up = [(i, (i + 1) % count) for i in range(count)]
    down = [(j, i) for i, j in up]
    here = lax.axis_index(axis)
    low, high = lax.ppermute(to_high, axis, up), lax.ppermute(to_low, axis, down)
    return jnp.where(here > 0, low, 0.0), jnp.where(here < count - 1, high, 0.0)


def call(kernel, outs, scratch=(), vmem=40 * 2**20, **kw):
    return pl.pallas_call(
        kernel,
        out_shape=outs,
        scratch_shapes=list(scratch),
        compiler_params=pltpu.CompilerParams(vmem_limit_bytes=vmem),
        **kw,
    )


def arr(*shape, dtype=F32):
    return jax.ShapeDtypeStruct(shape, dtype)


def parcels(recv, padded, weight):
    rows = padded.shape[0]
    nx = rows // ZR - 4
    blocks = recv.shape[0] // ROWS
    return call(
        parcel_kernel,
        [arr(5, 2 * blocks, LANES), arr(nx * ZR, LANES), arr(2 * ZR, LANES), arr(2 * ZR, LANES)],
        [
            pltpu.VMEM((8, LANES), jnp.int32),
            pltpu.SMEM((8, LANES), jnp.int32),
            pltpu.VMEM((rows, LANES), F32),
            pltpu.VMEM((rows, LANES), F32),
            pltpu.VMEM((8 * LANES, LANES), F32),
            pltpu.VMEM((8 * LANES, LANES), F32),
            pltpu.VMEM((5, 2 * blocks, LANES), F32),
            pltpu.SemaphoreType.DMA,
            pltpu.SemaphoreType.DMA,
        ],
        out_specs=[pl.BlockSpec(memory_space=pl.ANY)] + [pl.BlockSpec(memory_space=pltpu.VMEM)] * 3,
    )(recv, padded, weight)


def per_device(parcel_vel, parcel_props, fill_count, owner_peer, cell_offset, shell_weight, gas_state):
    _, nx, ny, nz = gas_state.shape
    blocks = parcel_vel.shape[0]
    x_low, x_high = shift_pair(gas_state[:, :2], gas_state[:, nx - 2 :], "gx", ring=True)
    send = call(
        pack_kernel,
        arr(blocks * ROWS, LANES),
        [pltpu.VMEM((1, blocks), jnp.int32)] * 3
        + [
            pltpu.VMEM((3, blocks, LANES), F32),
            pltpu.VMEM((blocks, 2, LANES), F32),
            pltpu.SemaphoreType.DMA((5,)),
        ],
        in_specs=[pl.BlockSpec(memory_space=pltpu.HBM)] * 5,
        vmem=NEARLY_ALL,
    )(
        owner_peer.reshape(1, blocks),
        cell_offset.reshape(1, blocks),
        fill_count.reshape(1, blocks),
        parcel_vel.transpose(1, 0, 2),
        parcel_props,
    )
    send, x_low, x_high = lax.optimization_barrier((send, x_low, x_high))
    recv = lax.all_to_all(
        send.reshape(blocks, ROWS * LANES), ("gx", "gy"), split_axis=0, concat_axis=0, tiled=True
    ).reshape(blocks * ROWS, LANES)
    planes = nx + 4
    rows_buf = [pltpu.VMEM((planes, LANES, nz), F32)]
    z_lo, z_hi = call(edge_kernel, [arr(planes, 2, LANES)] * 2, rows_buf)(gas_state, x_low, x_high)
    z_low, z_high = shift_pair(z_lo, z_hi, "gz")

    around = (gas_state, x_low, x_high, z_low, z_high)
    pairs = 4 * planes + planes // (SIDE // 2)
    y_lo, y_hi = call(yface_kernel, [arr(pairs, 2, nz)] * 2)(*around)
    y_low, y_high = shift_pair(y_lo, y_hi, "gy")
    padded = call(turn_kernel, arr(planes, ZR, LANES), rows_buf)(
        *around, y_low, y_high
    )

    weight = shell_weight.reshape(LANES, 4, 4, 8).transpose(2, 1, 3, 0).reshape(LANES, LANES)
    pay, total, x_lo, x_hi = parcels(recv, padded.reshape(planes * ZR, LANES), weight)
    parcels_next = pay.transpose(1, 0, 2)
    base = call(diffuse_kernel, arr(nx, nz, LANES))(padded)

    from_low, from_high = shift_pair(x_lo.reshape(2, ZR, LANES), x_hi.reshape(2, ZR, LANES), "gx", ring=True)
    total = total.reshape(nx, ZR, LANES)

    def rim(lo, hi):
        part = total[:, lo:hi]
        return jnp.concatenate(
            [part[:2] + from_low[:, lo:hi], part[2 : nx - 2], part[nx - 2 :] + from_high[:, lo:hi]], axis=0
        )

    z_below, z_above = shift_pair(rim(ZO - 2, ZO), rim(ZO + nz, ZO + nz + 2), "gz")
    rows_out, y_lo, y_hi = call(
        back_kernel,
        [arr(4, nx, ny, nz), arr(4, nx, 2, nz), arr(4, nx, 2, nz)],
        [pltpu.VMEM((nx, nz, LANES), F32)],
    )(total, base, from_low, from_high, z_below, z_above)
    y_below, y_above = shift_pair(y_lo, y_hi, "gy")
    gas_next = call(
        last_kernel,
        arr(4, nx, ny, nz),
        [pltpu.VMEM((4, nx, ny, nz), F32), pltpu.SemaphoreType.DMA((4,))],
        out_specs=pl.BlockSpec(memory_space=pl.ANY),
    )(rows_out, y_below, y_above)
    return parcels_next, gas_next


def solution(mesh):
    return jax.shard_map(
        per_device,
        mesh=mesh,
        in_specs=(
            P(("gx", "gy", "gz"), None, None),
            P(("gx", "gy", "gz"), None, None),
            P(("gx", "gy", "gz")),
            P(("gx", "gy", "gz"), None),
            P(("gx", "gy", "gz")),
            P(),
            P(None, "gx", "gy", "gz"),
        ),
        out_specs=(P(("gx", "gy", "gz"), None, None), P(None, "gx", "gy", "gz")),
        check_vma=False,
    )
```

```python
import functools
import jax
import jax.numpy as jnp
from jax import lax
from jax.experimental import pallas as pl
from jax.experimental.pallas import tpu as pltpu
from jax.sharding import PartitionSpec as P

TIME_STEP = 0.05
SETTLING = 1.0
F32 = jnp.float32
BF16 = jnp.bfloat16
HI = lax.Precision.HIGHEST

LANES = 128
NEARLY_ALL = 66200000
ROWS = 11
ZR = 144
ZO = 8
YS = 32


def iota(shape, dim):
    return lax.broadcasted_iota(jnp.int32, shape, dim)


def pack_kernel(
    tgt_hbm, off_hbm, cnt_hbm, vel_hbm, prop_hbm, out_hbm,
    tgt_ref, off_ref, cnt_ref, vel_ref, prop_ref, out_ref, sems, out_sems,
):
    n = LANES
    pairs = ((tgt_hbm, tgt_ref), (off_hbm, off_ref), (cnt_hbm, cnt_ref), (vel_hbm, vel_ref), (prop_hbm, prop_ref))
    copies = [pltpu.make_async_copy(src, dst, sems.at[i]) for i, (src, dst) in enumerate(pairs)]
    for copy in copies:
        copy.start()
    for copy in copies[:3]:
        copy.wait()
    hot = (iota((n, n), 0) == tgt_ref[...]).astype(F32)
    earlier = (iota((n, n), 0) < iota((n, n), 1)).astype(BF16)
    rank = jnp.dot(hot.astype(BF16), earlier, preferred_element_type=F32)
    first = jnp.where(rank < 0.5, hot, 0.0)
    second = jnp.where(rank > 0.5, hot, 0.0)
    off = off_ref[...].astype(F32)
    cnt = cnt_ref[...].astype(F32)
    lane = iota((n, n), 1)
    head = jnp.zeros((n, n), F32)
    for place, (pick, val) in enumerate(((first, off), (second, off), (first, cnt), (second, cnt))):
        column = jnp.sum(pick * val, axis=1, keepdims=True)
        head = jnp.where(lane == place, column, head)
    out_ref[pl.ds(10, n, stride=ROWS), :] = head
    for copy in copies[3:]:
        copy.wait()
    parts = []
    for k in range(5):
        x = vel_ref[k] if k < 3 else prop_ref[:, k - 3, :]
        high = x.astype(BF16)
        x = x - high.astype(F32)
        middle = x.astype(BF16)
        parts.append((jnp.concatenate([high, middle], axis=0), (x - middle.astype(F32)).astype(BF16)))
    half = n // 2
    leaving = []
    for h in range(2):
        lines = slice(h * half, (h + 1) * half)
        picks = jnp.concatenate([first[lines], second[lines]], axis=0).astype(BF16)
        picks_twice = jnp.concatenate([picks, picks], axis=1)
        at = h * half * ROWS
        for k, (upper, lower) in enumerate(parts):
            total = jnp.dot(picks_twice, upper, preferred_element_type=F32)
            total = total + jnp.dot(picks, lower, preferred_element_type=F32)
            out_ref[pl.ds(at + k, half, stride=ROWS), :] = total[:half]
            out_ref[pl.ds(at + 5 + k, half, stride=ROWS), :] = total[half:]
        block = pl.ds(at, half * ROWS)
        leaving.append(pltpu.make_async_copy(out_ref.at[block], out_hbm.at[block], out_sems.at[h]))
        leaving[-1].start()
    for copy in leaving:
        copy.wait()


def fill_rows(buf, gas_ref, xl_ref, xh_ref):
    cells_x, cells_y = gas_ref.shape[1], gas_ref.shape[2]
    for x in range(cells_x + 4):
        ref, at = (xl_ref, x) if x < 2 else (gas_ref, x - 2) if x < cells_x + 2 else (xh_ref, x - cells_x - 2)
        for k in range(4):
            buf[x, k * YS + 2 : k * YS + 2 + cells_y, :] = ref[k, at]


def edge_kernel(gas_ref, xl_ref, xh_ref, lo_ref, hi_ref, buf):
    cells_z = gas_ref.shape[3]
    buf[...] = jnp.zeros_like(buf)
    fill_rows(buf, gas_ref, xl_ref, xh_ref)
    for x in range(lo_ref.shape[0]):
        flat = buf[x].T
        lo_ref[x] = flat[0:2]
        hi_ref[x] = flat[cells_z - 2 : cells_z]


SIDE = 8


def yface_kernel(gas_ref, xl_ref, xh_ref, zl_ref, zh_ref, lo_ref, hi_ref):
    cells_x, cells_y = gas_ref.shape[1], gas_ref.shape[2]
    planes = cells_x + 4
    each = planes // (SIDE // 2)
    for ref, at in ((lo_ref, 0), (hi_ref, cells_y - 2)):
        for k in range(4):
            ref[k * planes : k * planes + 2] = xl_ref[k, :, at : at + 2, :]
            ref[k * planes + 2 : k * planes + 2 + cells_x] = gas_ref[k, :, at : at + 2, :]
            ref[k * planes + 2 + cells_x : (k + 1) * planes] = xh_ref[k, :, at : at + 2, :]
        total = None
        for m in range(SIDE):
            z_ref, first = (zl_ref, m) if m < SIDE // 2 else (zh_ref, m - SIDE // 2)
            rows = z_ref[first * each : (first + 1) * each].reshape(2 * each, LANES)
            rows = pltpu.roll(rows, (4 * m - 2 - at) % LANES, 1)
            y = iota(rows.shape, 1) % YS
            total = jnp.where((y >= 4 * m) & (y < 4 * m + 2), rows, 0.0 if total is None else total)
        ref[4 * planes : 4 * planes + each] = total.reshape(each, 2, LANES)


def turn_kernel(gas_ref, xl_ref, xh_ref, zl_ref, zh_ref, yl_ref, yh_ref, out_ref, buf):
    planes, cells_y, cells_z = out_ref.shape[0], gas_ref.shape[2], gas_ref.shape[3]
    each = planes // (SIDE // 2)
    buf[...] = jnp.zeros_like(buf)
    fill_rows(buf, gas_ref, xl_ref, xh_ref)
    for x in range(planes):
        for k in range(4):
            buf[x, k * YS : k * YS + 2, :] = yl_ref[k * planes + x]
            buf[x, k * YS + 2 + cells_y : k * YS + 4 + cells_y, :] = yh_ref[k * planes + x]
    below, above = (ref[4 * planes : 4 * planes + each].reshape(2 * each, LANES) for ref in (yl_ref, yh_ref))
    y = iota((2 * each, LANES), 1) % YS
    for m in range(SIDE):
        z_ref, first = (zl_ref, m) if m < SIDE // 2 else (zh_ref, m - SIDE // 2)
        inner = z_ref[first * each : (first + 1) * each].reshape(2 * each, LANES)
        low = pltpu.roll(below, -4 * m % LANES, 1)
        high = pltpu.roll(above, (2 + cells_y - 4 * m) % LANES, 1)
        rows = jnp.where(y < 2, low, jnp.where(y < 2 + cells_y, inner, jnp.where(y < 4 + cells_y, high, 0.0)))
        at = ZO - 2 if m < SIDE // 2 else ZO + cells_z
        for x in range(each):
            out_ref[first * each + x, at : at + 2, :] = rows[2 * x : 2 * x + 2]
    for x in range(planes):
        out_ref[x, ZO : ZO + cells_z, :] = buf[x].T


def diffuse_kernel(pad_ref, out_ref):
    cells_x, cells_z = out_ref.shape[0], out_ref.shape[1]
    last = ZO + cells_z
    lane = iota((cells_z, LANES), 1)
    rate = jnp.where(lane < 3 * YS, TIME_STEP, 0.5 * TIME_STEP).astype(F32)
    for x in range(2, cells_x + 2):
        here = pad_ref[x, ZO:last, :]
        beside = pad_ref[x - 1, ZO:last, :] + pad_ref[x + 1, ZO:last, :]
        beside = beside + pltpu.roll(here, LANES - 1, 1) + pltpu.roll(here, 1, 1)
        beside = beside + pad_ref[x, ZO + 1 : last + 1, :] + pad_ref[x, ZO - 1 : last - 1, :]
        out_ref[x - 2] = here + rate * (beside - 6.0 * here)


def parcel_kernel(
    recv_ref, pad, w_ref,
    pay_hbm, sum_ref, xlo_ref, xhi_ref,
    code_v, code_s, acc, more, near, force, pay_ref, sem, pay_sem,
):
    planes = pad.shape[0] // ZR
    n = LANES
    off = recv_ref[pl.ds(10, n, stride=ROWS), :]
    rest = jnp.floor((off + 0.5) * (1.0 / 125.0))
    oz = off - rest * 125.0
    ox = jnp.floor((rest + 0.5) * (1.0 / 17.0))
    oy = rest - ox * 17.0
    code = oy * 4096.0 + ox * float(ZR) + oz + float(ZO - 2)
    code_v[...] = code.T[0:8].astype(jnp.int32)
    copy = pltpu.make_async_copy(code_v, code_s, sem)
    copy.start()
    acc[...] = jnp.zeros_like(acc)
    more[...] = jnp.zeros_like(more)
    w_hi = w_ref[...].astype(BF16)
    w_lo = (w_ref[...] - w_hi.astype(F32)).astype(BF16)

    def split(x):
        hi = x.astype(BF16)
        return hi, (x - hi.astype(F32)).astype(BF16)

    copy.wait()

    lane8 = iota((8, n), 1)
    group = (lane8 % YS) // 4
    quad = lane8 % 4
    lane = iota((YS, n), 1)

    def place(s, b):
        c = code_s[s // 4, (s % 4) * YS + b]
        return jnp.bitwise_and(c, 4095), lax.shift_right_logical(c, 12)

    @pl.loop(0, 8, unroll=2)
    def _(s):
        merged = []
        for g in range(4):
            total = [None] * 4
            for b8 in range(8):
                at, oy_b = place(s, b8 * 4 + g)
                shift = jnp.bitwise_and(4 * b8 - oy_b, n - 1)
                mine = group == b8
                for a in range(4):
                    x = pltpu.roll(pad[pl.ds(at + a * ZR, 8), :], shift, 1)
                    total[a] = jnp.where(mine, x, 0.0 if total[a] is None else total[a])
            merged.append(total)
        cells = []
        for e in range(4):
            for a in range(4):
                x = merged[0][a]
                out = pltpu.roll(x, -e % n, 1) if e else x
                for g in range(1, 4):
                    x = merged[g][a]
                    x = pltpu.roll(x, (g - e) % n, 1) if g != e else x
                    out = jnp.where(quad == g, x, out)
                cells.append(out)
        near[pl.ds(pl.multiple_of(s * n, n), n), :] = jnp.concatenate(cells, axis=0).T

    near_hi, near_lo = split(near[...])
    gas_all = jnp.dot(
        jnp.concatenate([near_hi, near_lo], axis=1), jnp.concatenate([w_hi, w_hi], axis=0), preferred_element_type=F32
    ) + jnp.dot(near_hi, w_lo, preferred_element_type=F32)
    for s in range(8):
        rank, q0 = s // 4, (s % 4) * YS
        row = q0 * ROWS + rank * 5

        def take(k):
            return recv_ref[pl.ds(row + k, YS, stride=ROWS), :]

        head = recv_ref[pl.ds(q0 * ROWS + 10, YS, stride=ROWS), :]
        alive = lane.astype(F32) < head[:, 2 + rank : 3 + rank]
        mass = jnp.where(alive, take(3), 0.0)
        relax = jnp.where(alive, take(4), 1.0)
        drag = TIME_STEP / relax
        under = 1.0 / (1.0 + drag)
        slots = pl.ds(2 * q0 + rank, YS, stride=2)
        for k in range(3):
            gas = gas_all[s * n + k * YS : s * n + (k + 1) * YS]
            settle = TIME_STEP * SETTLING if k == 2 else 0.0
            vel = (take(k) + drag * gas - settle) * under
            force[s * n + k * YS : s * n + (k + 1) * YS, :] = -(mass * drag * (gas - vel))
            pay_ref[k, slots, :] = jnp.where(alive, vel, 0.0)
        pay_ref[3, slots, :] = mass
        pay_ref[4, slots, :] = jnp.where(alive, relax, 0.0)
        force[s * n + 3 * YS : (s + 1) * n, :] = mass
    leave = pltpu.make_async_copy(pay_ref, pay_hbm, pay_sem)
    leave.start()
    across = (((1,), (1,)), ((), ()))
    for s in range(8):
        f_hi, f_lo = split(force[s * n : (s + 1) * n, :])
        near[s * n : (s + 1) * n, :] = lax.dot_general(
            jnp.concatenate([w_hi, w_lo], axis=1),
            jnp.concatenate([f_hi, f_hi], axis=1),
            across,
            preferred_element_type=F32,
        ) + lax.dot_general(w_hi, f_lo, across, preferred_element_type=F32)

    @pl.loop(0, 8)
    def _(s):
        spread = near[pl.ds(pl.multiple_of(s * n, n), n), :]
        for g in range(4):
            parts = []
            for a in range(4):
                out = None
                for e in range(4):
                    x = spread[(e * 4 + a) * 8 : (e * 4 + a) * 8 + 8]
                    x = pltpu.roll(x, (e - g) % n, 1) if e != g else x
                    out = x if out is None else jnp.where(quad == e, x, out)
                parts.append(out)
            for b8 in range(0, 8, 2):
                work = []
                for half, sums in enumerate((acc, more)):
                    at, oy_b = place(s, (b8 + half) * 4 + g)
                    shift = jnp.bitwise_and(oy_b - 4 * (b8 + half), n - 1)
                    mine = group == b8 + half
                    for a in range(4):
                        add = pltpu.roll(jnp.where(mine, parts[a], 0.0), shift, 1)
                        work.append((sums, pl.ds(at + a * ZR, 8), add))
                olds = [sums[rows, :] for sums, rows, _ in work]
                for (sums, rows, add), old in zip(work, olds):
                    sums[rows, :] = old + add

    low, high = 2 * ZR, (planes - 2) * ZR
    sum_ref[...] = acc[low:high, :] + more[low:high, :]
    xlo_ref[...] = acc[0:low, :] + more[0:low, :]
    xhi_ref[...] = acc[high:, :] + more[high:, :]
    leave.wait()


def back_kernel(sum_ref, base_ref, xl_ref, xh_ref, zl_ref, zh_ref, out_ref, ylo_ref, yhi_ref, buf):
    cells_x = sum_ref.shape[0]
    cells_z = out_ref.shape[3]
    cells_y = out_ref.shape[2]
    for x in range(cells_x):
        value = sum_ref[x, ZO : ZO + cells_z, :]
        if x < 2:
            value = value + xl_ref[x, ZO : ZO + cells_z, :]
        if x >= cells_x - 2:
            value = value + xh_ref[x - cells_x + 2, ZO : ZO + cells_z, :]
        buf[x] = value
    buf[:, 0:2, :] += zl_ref[...]
    buf[:, cells_z - 2 : cells_z, :] += zh_ref[...]
    lane = iota((cells_z, LANES), 1)
    inside = (lane % YS >= 2) & (lane % YS < 2 + cells_y)
    for x in range(cells_x):
        flat = (buf[x] + jnp.where(inside, base_ref[x], 0.0)).T
        for k in range(4):
            out_ref[k, x] = flat[k * YS + 2 : k * YS + 2 + cells_y]
            ylo_ref[k, x] = flat[k * YS : k * YS + 2]
            yhi_ref[k, x] = flat[k * YS + 2 + cells_y : k * YS + 4 + cells_y]


def last_kernel(rows_ref, below_ref, above_ref, out_hbm, buf, sems):
    cells_y = rows_ref.shape[2]
    copies = []
    for k in range(4):
        buf[k] = rows_ref[k]
        buf[k, :, 0:2, :] += below_ref[k]
        buf[k, :, cells_y - 2 : cells_y, :] += above_ref[k]
        copies.append(pltpu.make_async_copy(buf.at[k], out_hbm.at[k], sems.at[k]))
        copies[-1].start()
    for copy in copies:
        copy.wait()


def shift_pair(to_low, to_high, axis, ring=False):
    count = lax.axis_size(axis)
    if not ring:
        up = [(i, i + 1) for i in range(count - 1)]
        down = [(j, i) for i, j in up]
        return lax.ppermute(to_high, axis, up), lax.ppermute(to_low, axis, down)
    up = [(i, (i + 1) % count) for i in range(count)]
    down = [(j, i) for i, j in up]
    here = lax.axis_index(axis)
    low, high = lax.ppermute(to_high, axis, up), lax.ppermute(to_low, axis, down)
    return jnp.where(here > 0, low, 0.0), jnp.where(here < count - 1, high, 0.0)


def call(kernel, outs, scratch=(), vmem=40 * 2**20, **kw):
    return pl.pallas_call(
        kernel,
        out_shape=outs,
        scratch_shapes=list(scratch),
        compiler_params=pltpu.CompilerParams(vmem_limit_bytes=vmem),
        **kw,
    )


def arr(*shape, dtype=F32):
    return jax.ShapeDtypeStruct(shape, dtype)


def parcels(recv, padded, weight):
    rows = padded.shape[0]
    nx = rows // ZR - 4
    blocks = recv.shape[0] // ROWS
    return call(
        parcel_kernel,
        [arr(5, 2 * blocks, LANES), arr(nx * ZR, LANES), arr(2 * ZR, LANES), arr(2 * ZR, LANES)],
        [
            pltpu.VMEM((8, LANES), jnp.int32),
            pltpu.SMEM((8, LANES), jnp.int32),
            pltpu.VMEM((rows, LANES), F32),
            pltpu.VMEM((rows, LANES), F32),
            pltpu.VMEM((8 * LANES, LANES), F32),
            pltpu.VMEM((8 * LANES, LANES), F32),
            pltpu.VMEM((5, 2 * blocks, LANES), F32),
            pltpu.SemaphoreType.DMA,
            pltpu.SemaphoreType.DMA,
        ],
        out_specs=[pl.BlockSpec(memory_space=pl.ANY)] + [pl.BlockSpec(memory_space=pltpu.VMEM)] * 3,
    )(recv, padded, weight)


def per_device(parcel_vel, parcel_props, fill_count, owner_peer, cell_offset, shell_weight, gas_state):
    _, nx, ny, nz = gas_state.shape
    blocks = parcel_vel.shape[0]
    x_low, x_high = shift_pair(gas_state[:, :2], gas_state[:, nx - 2 :], "gx", ring=True)
    send = call(
        pack_kernel,
        arr(blocks * ROWS, LANES),
        [pltpu.VMEM((1, blocks), jnp.int32)] * 3
        + [
            pltpu.VMEM((3, blocks, LANES), F32),
            pltpu.VMEM((blocks, 2, LANES), F32),
            pltpu.VMEM((blocks * ROWS, LANES), F32),
            pltpu.SemaphoreType.DMA((5,)),
            pltpu.SemaphoreType.DMA((2,)),
        ],
        in_specs=[pl.BlockSpec(memory_space=pltpu.HBM)] * 5,
        out_specs=pl.BlockSpec(memory_space=pltpu.HBM),
        vmem=NEARLY_ALL,
    )(
        owner_peer.reshape(1, blocks),
        cell_offset.reshape(1, blocks),
        fill_count.reshape(1, blocks),
        parcel_vel.transpose(1, 0, 2),
        parcel_props,
    )
    send, x_low, x_high = lax.optimization_barrier((send, x_low, x_high))
    recv = lax.all_to_all(
        send.reshape(blocks, ROWS * LANES), ("gx", "gy"), split_axis=0, concat_axis=0, tiled=True
    ).reshape(blocks * ROWS, LANES)
    planes = nx + 4
    rows_buf = [pltpu.VMEM((planes, LANES, nz), F32)]
    z_lo, z_hi = call(edge_kernel, [arr(planes, 2, LANES)] * 2, rows_buf)(gas_state, x_low, x_high)
    z_low, z_high = shift_pair(z_lo, z_hi, "gz")

    around = (gas_state, x_low, x_high, z_low, z_high)
    pairs = 4 * planes + planes // (SIDE // 2)
    y_lo, y_hi = call(yface_kernel, [arr(pairs, 2, nz)] * 2)(*around)
    y_low, y_high = shift_pair(y_lo, y_hi, "gy")
    padded = call(turn_kernel, arr(planes, ZR, LANES), rows_buf)(
        *around, y_low, y_high
    )

    weight = shell_weight.reshape(LANES, 4, 4, 8).transpose(2, 1, 3, 0).reshape(LANES, LANES)
    pay, total, x_lo, x_hi = parcels(recv, padded.reshape(planes * ZR, LANES), weight)
    parcels_next = pay.transpose(1, 0, 2)
    base = call(diffuse_kernel, arr(nx, nz, LANES))(padded)

    from_low, from_high = shift_pair(x_lo.reshape(2, ZR, LANES), x_hi.reshape(2, ZR, LANES), "gx", ring=True)
    total = total.reshape(nx, ZR, LANES)

    def rim(lo, hi):
        part = total[:, lo:hi]
        return jnp.concatenate(
            [part[:2] + from_low[:, lo:hi], part[2 : nx - 2], part[nx - 2 :] + from_high[:, lo:hi]], axis=0
        )

    z_below, z_above = shift_pair(rim(ZO - 2, ZO), rim(ZO + nz, ZO + nz + 2), "gz")
    rows_out, y_lo, y_hi = call(
        back_kernel,
        [arr(4, nx, ny, nz), arr(4, nx, 2, nz), arr(4, nx, 2, nz)],
        [pltpu.VMEM((nx, nz, LANES), F32)],
    )(total, base, from_low, from_high, z_below, z_above)
    y_below, y_above = shift_pair(y_lo, y_hi, "gy")
    gas_next = call(
        last_kernel,
        arr(4, nx, ny, nz),
        [pltpu.VMEM((4, nx, ny, nz), F32), pltpu.SemaphoreType.DMA((4,))],
        out_specs=pl.BlockSpec(memory_space=pl.ANY),
    )(rows_out, y_below, y_above)
    return parcels_next, gas_next


def solution(mesh):
    return jax.shard_map(
        per_device,
        mesh=mesh,
        in_specs=(
            P(("gx", "gy", "gz"), None, None),
            P(("gx", "gy", "gz"), None, None),
            P(("gx", "gy", "gz")),
            P(("gx", "gy", "gz"), None),
            P(("gx", "gy", "gz")),
            P(),
            P(None, "gx", "gy", "gz"),
        ),
        out_specs=(P(("gx", "gy", "gz"), None, None), P(None, "gx", "gy", "gz")),
        check_vma=False,
    )
```

```python
import functools
import jax
import jax.numpy as jnp
from jax import lax
from jax.experimental import pallas as pl
from jax.experimental.pallas import tpu as pltpu
from jax.sharding import PartitionSpec as P

TIME_STEP = 0.05
SETTLING = 1.0
F32 = jnp.float32
BF16 = jnp.bfloat16
HI = lax.Precision.HIGHEST

LANES = 128
NEARLY_ALL = 66200000
ROWS = 11
ZR = 144
ZO = 8
YS = 32


def iota(shape, dim):
    return lax.broadcasted_iota(jnp.int32, shape, dim)


def pack_kernel(
    tgt_hbm, off_hbm, cnt_hbm, vel_hbm, prop_hbm, out_hbm,
    tgt_ref, off_ref, cnt_ref, vel_ref, prop_ref, out_ref, sems, out_sems,
):
    n = LANES
    pairs = ((tgt_hbm, tgt_ref), (off_hbm, off_ref), (cnt_hbm, cnt_ref), (vel_hbm, vel_ref), (prop_hbm, prop_ref))
    copies = [pltpu.make_async_copy(src, dst, sems.at[i]) for i, (src, dst) in enumerate(pairs)]
    for copy in copies:
        copy.start()
    for copy in copies[:3]:
        copy.wait()
    hot = (iota((n, n), 0) == tgt_ref[...]).astype(F32)
    earlier = (iota((n, n), 0) < iota((n, n), 1)).astype(BF16)
    rank = jnp.dot(hot.astype(BF16), earlier, preferred_element_type=F32)
    first = jnp.where(rank < 0.5, hot, 0.0)
    second = jnp.where(rank > 0.5, hot, 0.0)
    off = off_ref[...].astype(F32)
    cnt = cnt_ref[...].astype(F32)
    lane = iota((n, n), 1)
    head = jnp.zeros((n, n), F32)
    for place, (pick, val) in enumerate(((first, off), (second, off), (first, cnt), (second, cnt))):
        column = jnp.sum(pick * val, axis=1, keepdims=True)
        head = jnp.where(lane == place, column, head)
    out_ref[pl.ds(10, n, stride=ROWS), :] = head
    for copy in copies[3:]:
        copy.wait()
    parts = []
    for k in range(5):
        x = vel_ref[k] if k < 3 else prop_ref[:, k - 3, :]
        high = x.astype(BF16)
        x = x - high.astype(F32)
        middle = x.astype(BF16)
        parts.append((jnp.concatenate([high, middle], axis=0), (x - middle.astype(F32)).astype(BF16)))
    half = n // 2
    leaving = []
    for h in range(2):
        lines = slice(h * half, (h + 1) * half)
        picks = jnp.concatenate([first[lines], second[lines]], axis=0).astype(BF16)
        picks_twice = jnp.concatenate([picks, picks], axis=1)
        at = h * half * ROWS
        for k, (upper, lower) in enumerate(parts):
            total = jnp.dot(picks_twice, upper, preferred_element_type=F32)
            total = total + jnp.dot(picks, lower, preferred_element_type=F32)
            out_ref[pl.ds(at + k, half, stride=ROWS), :] = total[:half]
            out_ref[pl.ds(at + 5 + k, half, stride=ROWS), :] = total[half:]
        block = pl.ds(at, half * ROWS)
        leaving.append(pltpu.make_async_copy(out_ref.at[block], out_hbm.at[block], out_sems.at[h]))
        leaving[-1].start()
    for copy in leaving:
        copy.wait()


def fill_rows(buf, gas_ref, xl_ref, xh_ref):
    cells_x, cells_y = gas_ref.shape[1], gas_ref.shape[2]
    for x in range(cells_x + 4):
        ref, at = (xl_ref, x) if x < 2 else (gas_ref, x - 2) if x < cells_x + 2 else (xh_ref, x - cells_x - 2)
        for k in range(4):
            buf[x, k * YS + 2 : k * YS + 2 + cells_y, :] = ref[k, at]


def edge_kernel(gas_ref, xl_ref, xh_ref, lo_ref, hi_ref, buf):
    cells_z = gas_ref.shape[3]
    buf[...] = jnp.zeros_like(buf)
    fill_rows(buf, gas_ref, xl_ref, xh_ref)
    for x in range(lo_ref.shape[0]):
        flat = buf[x].T
        lo_ref[x] = flat[0:2]
        hi_ref[x] = flat[cells_z - 2 : cells_z]


SIDE = 8


def yface_kernel(gas_ref, xl_ref, xh_ref, zl_ref, zh_ref, lo_ref, hi_ref):
    cells_x, cells_y = gas_ref.shape[1], gas_ref.shape[2]
    planes = cells_x + 4
    each = planes // (SIDE // 2)
    for ref, at in ((lo_ref, 0), (hi_ref, cells_y - 2)):
        for k in range(4):
            ref[k * planes : k * planes + 2] = xl_ref[k, :, at : at + 2, :]
            ref[k * planes + 2 : k * planes + 2 + cells_x] = gas_ref[k, :, at : at + 2, :]
            ref[k * planes + 2 + cells_x : (k + 1) * planes] = xh_ref[k, :, at : at + 2, :]
        total = None
        for m in range(SIDE):
            z_ref, first = (zl_ref, m) if m < SIDE // 2 else (zh_ref, m - SIDE // 2)
            rows = z_ref[first * each : (first + 1) * each].reshape(2 * each, LANES)
            rows = pltpu.roll(rows, (4 * m - 2 - at) % LANES, 1)
            y = iota(rows.shape, 1) % YS
            total = jnp.where((y >= 4 * m) & (y < 4 * m + 2), rows, 0.0 if total is None else total)
        ref[4 * planes : 4 * planes + each] = total.reshape(each, 2, LANES)


def turn_kernel(gas_ref, xl_ref, xh_ref, zl_ref, zh_ref, yl_ref, yh_ref, out_ref, buf):
    planes, cells_y, cells_z = out_ref.shape[0], gas_ref.shape[2], gas_ref.shape[3]
    each = planes // (SIDE // 2)
    buf[...] = jnp.zeros_like(buf)
    fill_rows(buf, gas_ref, xl_ref, xh_ref)
    for x in range(planes):
        for k in range(4):
            buf[x, k * YS : k * YS + 2, :] = yl_ref[k * planes + x]
            buf[x, k * YS + 2 + cells_y : k * YS + 4 + cells_y, :] = yh_ref[k * planes + x]
    below, above = (ref[4 * planes : 4 * planes + each].reshape(2 * each, LANES) for ref in (yl_ref, yh_ref))
    y = iota((2 * each, LANES), 1) % YS
    for m in range(SIDE):
        z_ref, first = (zl_ref, m) if m < SIDE // 2 else (zh_ref, m - SIDE // 2)
        inner = z_ref[first * each : (first + 1) * each].reshape(2 * each, LANES)
        low = pltpu.roll(below, -4 * m % LANES, 1)
        high = pltpu.roll(above, (2 + cells_y - 4 * m) % LANES, 1)
        rows = jnp.where(y < 2, low, jnp.where(y < 2 + cells_y, inner, jnp.where(y < 4 + cells_y, high, 0.0)))
        at = ZO - 2 if m < SIDE // 2 else ZO + cells_z
        for x in range(each):
            out_ref[first * each + x, at : at + 2, :] = rows[2 * x : 2 * x + 2]
    for x in range(planes):
        out_ref[x, ZO : ZO + cells_z, :] = buf[x].T


def diffuse_kernel(pad_ref, out_ref):
    cells_x, cells_z = out_ref.shape[0], out_ref.shape[1]
    last = ZO + cells_z
    lane = iota((cells_z, LANES), 1)
    rate = jnp.where(lane < 3 * YS, TIME_STEP, 0.5 * TIME_STEP).astype(F32)
    for x in range(2, cells_x + 2):
        here = pad_ref[x, ZO:last, :]
        beside = pad_ref[x - 1, ZO:last, :] + pad_ref[x + 1, ZO:last, :]
        beside = beside + pltpu.roll(here, LANES - 1, 1) + pltpu.roll(here, 1, 1)
        beside = beside + pad_ref[x, ZO + 1 : last + 1, :] + pad_ref[x, ZO - 1 : last - 1, :]
        out_ref[x - 2] = here + rate * (beside - 6.0 * here)


def parcel_kernel(
    recv_ref, pad, w_ref,
    pay_hbm, sum_ref, xlo_ref, xhi_ref,
    code_v, code_s, acc, more, near, force, ready, pay_ref, sem, pay_sem,
):
    planes = pad.shape[0] // ZR
    n = LANES
    off = recv_ref[pl.ds(10, n, stride=ROWS), :]
    rest = jnp.floor((off + 0.5) * (1.0 / 125.0))
    oz = off - rest * 125.0
    ox = jnp.floor((rest + 0.5) * (1.0 / 17.0))
    oy = rest - ox * 17.0
    code = oy * 4096.0 + ox * float(ZR) + oz + float(ZO - 2)
    code_v[...] = code.T[0:8].astype(jnp.int32)
    copy = pltpu.make_async_copy(code_v, code_s, sem)
    copy.start()
    acc[...] = jnp.zeros_like(acc)
    more[...] = jnp.zeros_like(more)
    w_hi = w_ref[...].astype(BF16)
    w_lo = (w_ref[...] - w_hi.astype(F32)).astype(BF16)

    def split(x):
        hi = x.astype(BF16)
        return hi, (x - hi.astype(F32)).astype(BF16)

    lane = iota((YS, n), 1)
    for s in range(8):
        rank, q0 = s // 4, (s % 4) * YS
        row = q0 * ROWS + rank * 5

        def take(k):
            return recv_ref[pl.ds(row + k, YS, stride=ROWS), :]

        alive = lane.astype(F32) < recv_ref[pl.ds(q0 * ROWS + 10, YS, stride=ROWS), :][:, 2 + rank : 3 + rank]
        mass = jnp.where(alive, take(3), 0.0)
        relax = jnp.where(alive, take(4), 1.0)
        drag = TIME_STEP / relax
        under = jnp.where(alive, 1.0 / (1.0 + drag), 0.0)
        mine = slice(s * YS, (s + 1) * YS)
        slots = pl.ds(2 * q0 + rank, YS, stride=2)
        for k in range(3):
            settle = TIME_STEP * SETTLING if k == 2 else 0.0
            ready[k, mine, :] = (take(k) - settle) * under
        ready[3, mine, :] = drag * under
        ready[4, mine, :] = mass * drag
        pay_ref[3, slots, :] = mass
        pay_ref[4, slots, :] = jnp.where(alive, relax, 0.0)
        force[s * n + 3 * YS : (s + 1) * n, :] = mass
    copy.wait()

    lane8 = iota((8, n), 1)
    group = (lane8 % YS) // 4
    quad = lane8 % 4

    def place(s, b):
        c = code_s[s // 4, (s % 4) * YS + b]
        return jnp.bitwise_and(c, 4095), lax.shift_right_logical(c, 12)

    @pl.loop(0, 8, unroll=2)
    def _(s):
        merged = []
        for g in range(4):
            total = [None] * 4
            for b8 in range(8):
                at, oy_b = place(s, b8 * 4 + g)
                shift = jnp.bitwise_and(4 * b8 - oy_b, n - 1)
                mine = group == b8
                for a in range(4):
                    x = pltpu.roll(pad[pl.ds(at + a * ZR, 8), :], shift, 1)
                    total[a] = jnp.where(mine, x, 0.0 if total[a] is None else total[a])
            merged.append(total)
        cells = []
        for e in range(4):
            for a in range(4):
                x = merged[0][a]
                out = pltpu.roll(x, -e % n, 1) if e else x
                for g in range(1, 4):
                    x = merged[g][a]
                    x = pltpu.roll(x, (g - e) % n, 1) if g != e else x
                    out = jnp.where(quad == g, x, out)
                cells.append(out)
        near[pl.ds(pl.multiple_of(s * n, n), n), :] = jnp.concatenate(cells, axis=0).T

    near_hi, near_lo = split(near[...])
    gas_all = jnp.dot(
        jnp.concatenate([near_hi, near_lo], axis=1), jnp.concatenate([w_hi, w_hi], axis=0), preferred_element_type=F32
    ) + jnp.dot(near_hi, w_lo, preferred_element_type=F32)
    for s in range(8):
        slots = pl.ds(2 * (s % 4) * YS + s // 4, YS, stride=2)
        mine = slice(s * YS, (s + 1) * YS)
        share, push = ready[3, mine, :], ready[4, mine, :]
        for k in range(3):
            rows = slice(s * n + k * YS, s * n + (k + 1) * YS)
            gas = gas_all[rows]
            vel = ready[k, mine, :] + share * gas
            force[rows, :] = push * (vel - gas)
            pay_ref[k, slots, :] = vel
    leave = pltpu.make_async_copy(pay_ref, pay_hbm, pay_sem)
    leave.start()
    across = (((1,), (1,)), ((), ()))
    for s in range(8):
        f_hi, f_lo = split(force[s * n : (s + 1) * n, :])
        near[s * n : (s + 1) * n, :] = lax.dot_general(
            jnp.concatenate([w_hi, w_lo], axis=1),
            jnp.concatenate([f_hi, f_hi], axis=1),
            across,
            preferred_element_type=F32,
        ) + lax.dot_general(w_hi, f_lo, across, preferred_element_type=F32)

    @pl.loop(0, 8)
    def _(s):
        spread = near[pl.ds(pl.multiple_of(s * n, n), n), :]
        for g in range(4):
            parts = []
            for a in range(4):
                out = None
                for e in range(4):
                    x = spread[(e * 4 + a) * 8 : (e * 4 + a) * 8 + 8]
                    x = pltpu.roll(x, (e - g) % n, 1) if e != g else x
                    out = x if out is None else jnp.where(quad == e, x, out)
                parts.append(out)
            for b8 in range(0, 8, 2):
                work = []
                for half, sums in enumerate((acc, more)):
                    at, oy_b = place(s, (b8 + half) * 4 + g)
                    shift = jnp.bitwise_and(oy_b - 4 * (b8 + half), n - 1)
                    mine = group == b8 + half
                    for a in range(4):
                        add = pltpu.roll(jnp.where(mine, parts[a], 0.0), shift, 1)
                        work.append((sums, pl.ds(at + a * ZR, 8), add))
                olds = [sums[rows, :] for sums, rows, _ in work]
                for (sums, rows, add), old in zip(work, olds):
                    sums[rows, :] = old + add

    low, high = 2 * ZR, (planes - 2) * ZR
    sum_ref[...] = acc[low:high, :] + more[low:high, :]
    xlo_ref[...] = acc[0:low, :] + more[0:low, :]
    xhi_ref[...] = acc[high:, :] + more[high:, :]
    leave.wait()


def back_kernel(sum_ref, base_ref, xl_ref, xh_ref, zl_ref, zh_ref, out_ref, ylo_ref, yhi_ref, buf):
    cells_x = sum_ref.shape[0]
    cells_z = out_ref.shape[3]
    cells_y = out_ref.shape[2]
    for x in range(cells_x):
        value = sum_ref[x, ZO : ZO + cells_z, :]
        if x < 2:
            value = value + xl_ref[x, ZO : ZO + cells_z, :]
        if x >= cells_x - 2:
            value = value + xh_ref[x - cells_x + 2, ZO : ZO + cells_z, :]
        buf[x] = value
    buf[:, 0:2, :] += zl_ref[...]
    buf[:, cells_z - 2 : cells_z, :] += zh_ref[...]
    lane = iota((cells_z, LANES), 1)
    inside = (lane % YS >= 2) & (lane % YS < 2 + cells_y)
    for x in range(cells_x):
        flat = (buf[x] + jnp.where(inside, base_ref[x], 0.0)).T
        for k in range(4):
            out_ref[k, x] = flat[k * YS + 2 : k * YS + 2 + cells_y]
            ylo_ref[k, x] = flat[k * YS : k * YS + 2]
            yhi_ref[k, x] = flat[k * YS + 2 + cells_y : k * YS + 4 + cells_y]


def last_kernel(rows_ref, below_ref, above_ref, out_hbm, buf, sems):
    cells_y = rows_ref.shape[2]
    copies = []
    for k in range(4):
        buf[k] = rows_ref[k]
        buf[k, :, 0:2, :] += below_ref[k]
        buf[k, :, cells_y - 2 : cells_y, :] += above_ref[k]
        copies.append(pltpu.make_async_copy(buf.at[k], out_hbm.at[k], sems.at[k]))
        copies[-1].start()
    for copy in copies:
        copy.wait()


def shift_pair(to_low, to_high, axis, ring=False):
    count = lax.axis_size(axis)
    if not ring:
        up = [(i, i + 1) for i in range(count - 1)]
        down = [(j, i) for i, j in up]
        return lax.ppermute(to_high, axis, up), lax.ppermute(to_low, axis, down)
    up = [(i, (i + 1) % count) for i in range(count)]
    down = [(j, i) for i, j in up]
    here = lax.axis_index(axis)
    low, high = lax.ppermute(to_high, axis, up), lax.ppermute(to_low, axis, down)
    return jnp.where(here > 0, low, 0.0), jnp.where(here < count - 1, high, 0.0)


def call(kernel, outs, scratch=(), vmem=40 * 2**20, **kw):
    return pl.pallas_call(
        kernel,
        out_shape=outs,
        scratch_shapes=list(scratch),
        compiler_params=pltpu.CompilerParams(vmem_limit_bytes=vmem),
        **kw,
    )


def arr(*shape, dtype=F32):
    return jax.ShapeDtypeStruct(shape, dtype)


def parcels(recv, padded, weight):
    rows = padded.shape[0]
    nx = rows // ZR - 4
    blocks = recv.shape[0] // ROWS
    return call(
        parcel_kernel,
        [arr(5, 2 * blocks, LANES), arr(nx * ZR, LANES), arr(2 * ZR, LANES), arr(2 * ZR, LANES)],
        [
            pltpu.VMEM((8, LANES), jnp.int32),
            pltpu.SMEM((8, LANES), jnp.int32),
            pltpu.VMEM((rows, LANES), F32),
            pltpu.VMEM((rows, LANES), F32),
            pltpu.VMEM((8 * LANES, LANES), F32),
            pltpu.VMEM((8 * LANES, LANES), F32),
            pltpu.VMEM((5, 2 * blocks, LANES), F32),
            pltpu.VMEM((5, 2 * blocks, LANES), F32),
            pltpu.SemaphoreType.DMA,
            pltpu.SemaphoreType.DMA,
        ],
        out_specs=[pl.BlockSpec(memory_space=pl.ANY)] + [pl.BlockSpec(memory_space=pltpu.VMEM)] * 3,
    )(recv, padded, weight)


def per_device(parcel_vel, parcel_props, fill_count, owner_peer, cell_offset, shell_weight, gas_state):
    _, nx, ny, nz = gas_state.shape
    blocks = parcel_vel.shape[0]
    x_low, x_high = shift_pair(gas_state[:, :2], gas_state[:, nx - 2 :], "gx", ring=True)
    send = call(
        pack_kernel,
        arr(blocks * ROWS, LANES),
        [pltpu.VMEM((1, blocks), jnp.int32)] * 3
        + [
            pltpu.VMEM((3, blocks, LANES), F32),
            pltpu.VMEM((blocks, 2, LANES), F32),
            pltpu.VMEM((blocks * ROWS, LANES), F32),
            pltpu.SemaphoreType.DMA((5,)),
            pltpu.SemaphoreType.DMA((2,)),
        ],
        in_specs=[pl.BlockSpec(memory_space=pltpu.HBM)] * 5,
        out_specs=pl.BlockSpec(memory_space=pltpu.HBM),
        vmem=NEARLY_ALL,
    )(
        owner_peer.reshape(1, blocks),
        cell_offset.reshape(1, blocks),
        fill_count.reshape(1, blocks),
        parcel_vel.transpose(1, 0, 2),
        parcel_props,
    )
    send, x_low, x_high = lax.optimization_barrier((send, x_low, x_high))
    recv = lax.all_to_all(
        send.reshape(blocks, ROWS * LANES), ("gx", "gy"), split_axis=0, concat_axis=0, tiled=True
    ).reshape(blocks * ROWS, LANES)
    planes = nx + 4
    rows_buf = [pltpu.VMEM((planes, LANES, nz), F32)]
    z_lo, z_hi = call(edge_kernel, [arr(planes, 2, LANES)] * 2, rows_buf)(gas_state, x_low, x_high)
    z_low, z_high = shift_pair(z_lo, z_hi, "gz")

    around = (gas_state, x_low, x_high, z_low, z_high)
    pairs = 4 * planes + planes // (SIDE // 2)
    y_lo, y_hi = call(yface_kernel, [arr(pairs, 2, nz)] * 2)(*around)
    y_low, y_high = shift_pair(y_lo, y_hi, "gy")
    padded = call(turn_kernel, arr(planes, ZR, LANES), rows_buf)(
        *around, y_low, y_high
    )

    weight = shell_weight.reshape(LANES, 4, 4, 8).transpose(2, 1, 3, 0).reshape(LANES, LANES)
    pay, total, x_lo, x_hi = parcels(recv, padded.reshape(planes * ZR, LANES), weight)
    parcels_next = pay.transpose(1, 0, 2)
    base = call(diffuse_kernel, arr(nx, nz, LANES))(padded)

    from_low, from_high = shift_pair(x_lo.reshape(2, ZR, LANES), x_hi.reshape(2, ZR, LANES), "gx", ring=True)
    total = total.reshape(nx, ZR, LANES)

    def rim(lo, hi):
        part = total[:, lo:hi]
        return jnp.concatenate(
            [part[:2] + from_low[:, lo:hi], part[2 : nx - 2], part[nx - 2 :] + from_high[:, lo:hi]], axis=0
        )

    z_below, z_above = shift_pair(rim(ZO - 2, ZO), rim(ZO + nz, ZO + nz + 2), "gz")
    rows_out, y_lo, y_hi = call(
        back_kernel,
        [arr(4, nx, ny, nz), arr(4, nx, 2, nz), arr(4, nx, 2, nz)],
        [pltpu.VMEM((nx, nz, LANES), F32)],
    )(total, base, from_low, from_high, z_below, z_above)
    y_below, y_above = shift_pair(y_lo, y_hi, "gy")
    gas_next = call(
        last_kernel,
        arr(4, nx, ny, nz),
        [pltpu.VMEM((4, nx, ny, nz), F32), pltpu.SemaphoreType.DMA((4,))],
        out_specs=pl.BlockSpec(memory_space=pl.ANY),
    )(rows_out, y_below, y_above)
    return parcels_next, gas_next


def solution(mesh):
    return jax.shard_map(
        per_device,
        mesh=mesh,
        in_specs=(
            P(("gx", "gy", "gz"), None, None),
            P(("gx", "gy", "gz"), None, None),
            P(("gx", "gy", "gz")),
            P(("gx", "gy", "gz"), None),
            P(("gx", "gy", "gz")),
            P(),
            P(None, "gx", "gy", "gz"),
        ),
        out_specs=(P(("gx", "gy", "gz"), None, None), P(None, "gx", "gy", "gz")),
        check_vma=False,
    )
```
